512 devices in a mesh: rows: 64 (over y, z), cols: 8 (over x, core).
Axes of the slice: x: 4, y: 4, z: 16, core: 2. Of those that a mesh axis runs over, the one named last changes fastest.
Arguments:
- queries: bfloat16 [9216, 768], P('rows', 'cols'), may hold values from -4 to 4
- passages: bfloat16 [9216, 768], P('cols', 'rows'), may hold values from -2 to 2
- positive: int32 [9216], P('rows'), may hold values from 0 to 9215, each once
Outputs:
- query_grad: float32 [9216, 768], P('rows', 'cols')
- passage_grad: float32 [9216, 768], P('cols', 'rows')
The draws below stay inside these ranges and needn't reach their ends.
Inputs may be any that keep to these rules, and one draw needn't show every extreme that they name: Every passage is the positive of exactly one query.
All inputs are finite; a program needn't handle non-finite values.
Results may differ from the reference program's by a relative error of at most 0.002.
Values may be sent and summed in bfloat16 or wider, within the bound.
No kernel may reach another device: no remote copies, remote signals or barrier semaphores. Data moves between devices by JAX's collectives and lax.ppermute only.
A program may use at most 64 MiB of HBM per device.

```python
import math
import jax
import jax.numpy as jnp
from jax import lax

D = 768
B = 9216


def row_scales(key, low, high):
    return jnp.exp(jax.random.uniform(key, (B,), jnp.float32, math.log(low), math.log(high)))


def draw_queries(key, part):
    key = jax.random.fold_in(key, 11)
    key_noise, key_scale = jax.random.split(key, 2)
    ramp_up = 0.5 + jnp.arange(B, dtype=jnp.float32) / B
    noise = jnp.clip(jax.random.normal(key_noise, (B, D), jnp.float32), -6.0, 6.0)
    scales = row_scales(key_scale, 0.3, 3.0)
    values = noise * (scales * ramp_up)[:, None] / math.sqrt(D)
    return jnp.clip(values, -4.0, 4.0).astype(jnp.bfloat16)


def draw_passages(key, part):
    key = jax.random.fold_in(key, 23)
    key_noise, key_scale = jax.random.split(key, 2)
    ramp_up = 0.5 + jnp.arange(B, dtype=jnp.float32) / B
    noise = jnp.clip(jax.random.normal(key_noise, (B, D), jnp.float32), -6.0, 6.0)
    scales = row_scales(key_scale, 0.3, 3.0)
    values = noise * (scales * ramp_up)[:, None] / math.sqrt(D)
    return jnp.clip(values, -2.0, 2.0).astype(jnp.bfloat16)


def setup_inputs(seed: int = 0) -> dict:
    key_list = jax.random.split(jax.random.key(seed), 4)
    return {
        "queries": draw_queries(jax.random.fold_in(key_list[3], 71), 0),
        "passages": draw_passages(jax.random.fold_in(key_list[3], 71), 0),
        "positive": jax.random.permutation(key_list[2], B).astype(jnp.int32),
    }


logit_scale = 20.0

def score_block(query_block, passage_block):
    return logit_scale * jnp.dot(query_block, passage_block.T, preferred_element_type=jnp.float32)

def log_total(scores, axis_id):
    peak = lax.optimization_barrier(jnp.max(scores, axis=axis_id, keepdims=True))
    total = lax.optimization_barrier(jnp.sum(jnp.exp(scores - peak), axis=axis_id, keepdims=True))
    return jnp.squeeze(peak + jnp.log(total), axis=axis_id)

def reference(queries, passages, positive):
    block_rows = math_block(B)
    nblocks = B // block_rows
    query_blocks = queries.reshape(nblocks, block_rows, D)
    passage_blocks = passages.reshape(nblocks, block_rows, D)
    column_ids = jnp.arange(B, dtype=jnp.int32)
    row_lse = lax.map(lambda qb: log_total(score_block(qb, passages), 1), query_blocks).reshape(B)
    col_lse = lax.map(lambda pb: log_total(score_block(queries, pb), 0), passage_blocks).reshape(B)

    def rows_grad(args):
        qb, pos_block, lse_block = args
        scores = score_block(qb, passages)
        hit = (pos_block[:, None] == column_ids[None, :]).astype(jnp.float32)
        dlogits = (jnp.exp(scores - lse_block[:, None]) + jnp.exp(scores - col_lse[None, :]) - 2.0 * hit).astype(jnp.bfloat16)
        return logit_scale * jnp.dot(dlogits, passages, preferred_element_type=jnp.float32)

    def cols_grad(args):
        pb, id_block, lse_block = args
        scores = score_block(queries, pb)
        hit = (positive[:, None] == id_block[None, :]).astype(jnp.float32)
        dlogits = (jnp.exp(scores - row_lse[:, None]) + jnp.exp(scores - lse_block[None, :]) - 2.0 * hit).astype(jnp.bfloat16)
        return logit_scale * jnp.dot(dlogits.T, queries, preferred_element_type=jnp.float32)
    query_grad = lax.map(rows_grad, (query_blocks, positive.reshape(nblocks, block_rows), row_lse.reshape(nblocks, block_rows))).reshape(B, D)
    passage_grad = lax.map(cols_grad, (passage_blocks, column_ids.reshape(nblocks, block_rows), col_lse.reshape(nblocks, block_rows))).reshape(B, D)
    return (query_grad, passage_grad)

def math_block(total):
    block = 512
    while total % block != 0:
        block = block // 2
    return block
```

```python
import jax
import jax.numpy as jnp
from jax import lax
from jax.sharding import Mesh, PartitionSpec as P

logit_scale = 20.0
f32 = jnp.float32
bf16 = jnp.bfloat16


def share(x, axes, n):
    return lax.all_to_all(jnp.broadcast_to(x[None], (n, *x.shape)), axes, 0, 0, tiled=True)


def merge(pairs):
    top = jnp.max(pairs[:, 0], axis=0)
    total = jnp.sum(pairs[:, 1] * jnp.exp(pairs[:, 0] - top[None]), axis=0)
    return jnp.stack([top, total])


def body(queries, passages, positive):
    rows, width = queries.shape
    cols, slice_width = passages.shape
    query_parts = share(queries, ("x", "core"), 8)
    query_full = query_parts.transpose(1, 0, 2).reshape(rows, 8 * width)
    part = lax.all_gather(passages.T, "z", axis=0, tiled=False).reshape(16 * slice_width, cols)
    passage_full = share(part, "y", 4).reshape(64 * slice_width, cols)

    logit_tile = logit_scale * jnp.dot(query_full, passage_full, preferred_element_type=f32)
    row_top = jnp.max(logit_tile, axis=1)
    row_sum = jnp.sum(jnp.exp(logit_tile - row_top[:, None]), axis=1)
    col_top = jnp.max(logit_tile, axis=0)
    col_sum = jnp.sum(jnp.exp(logit_tile - col_top[None, :]), axis=0)
    row_pair = merge(share(jnp.stack([row_top, row_sum]), ("x", "core"), 8))
    col_pair = merge(share(jnp.stack([col_top, col_sum]), "y", 4))
    col_pair = merge(share(col_pair, "z", 16))
    row_lse = row_pair[0] + jnp.log(row_pair[1])
    col_lse = col_pair[0] + jnp.log(col_pair[1])

    block = lax.axis_index("x") * 2 + lax.axis_index("core")
    column_ids = block * cols + jnp.arange(cols, dtype=jnp.int32)
    hit = (positive[:, None] == column_ids[None, :]).astype(f32)
    dlogits = (
        jnp.exp(logit_tile - row_lse[:, None]) + jnp.exp(logit_tile - col_lse[None, :]) - 2.0 * hit
    ).astype(bf16)

    passage_terms = logit_scale * lax.dot_general(
        query_full, dlogits, (((0,), (0,)), ((), ())), preferred_element_type=f32
    )
    passage_terms = passage_terms.astype(bf16).reshape(4, 16 * slice_width, cols)
    passage_terms = lax.all_to_all(passage_terms, "y", 0, 0, tiled=True)
    passage_terms = jnp.sum(passage_terms.astype(f32), axis=0)
    passage_terms = lax.all_to_all(passage_terms.reshape(16, slice_width, cols), "z", 0, 0, tiled=True)
    passage_grad = jnp.sum(passage_terms, axis=0).T

    query_terms = logit_scale * lax.dot_general(
        dlogits, passage_full, (((1,), (1,)), ((), ())), preferred_element_type=f32
    )
    query_terms = query_terms.astype(bf16).reshape(rows, 8, width).transpose(1, 0, 2)
    query_terms = lax.all_to_all(query_terms, ("x", "core"), 0, 0, tiled=True)
    query_grad = jnp.sum(query_terms.astype(f32), axis=0)
    return (query_grad, passage_grad)


def solution(mesh):
    chips = Mesh(mesh.devices.reshape(4, 16, 4, 2), ("y", "z", "x", "core"))
    yz, xc = ("y", "z"), ("x", "core")
    return jax.shard_map(
        body,
        mesh=chips,
        in_specs=(P(yz, xc), P(xc, yz), P(yz)),
        out_specs=(P(yz, xc), P(xc, yz)),
        check_vma=False,
    )
```

```python
import jax
import jax.numpy as jnp
import numpy as np
from jax import lax
from jax.sharding import Mesh, PartitionSpec as P

logit_scale = 20.0
f32 = jnp.float32
bf16 = jnp.bfloat16
NY, NZ, NX, NC = 4, 16, 4, 2
SHORT = ("y", "x", "core")


def share(x, axes, n):
    return lax.all_to_all(jnp.broadcast_to(x[None], (n, *x.shape)), axes, 0, 0, tiled=True)


def merge(pairs):
    top = jnp.max(pairs[:, 0], axis=0)
    total = jnp.sum(pairs[:, 1] * jnp.exp(pairs[:, 0] - top[None]), axis=0)
    return top + jnp.log(total)


def placement(slice_width, width):
    table = np.zeros((NX * NC, 128, NZ, NY, slice_width), np.float32)
    for d in range(NX * NC * width):
        y, z, k = d // (NZ * slice_width), d // slice_width % NZ, d % slice_width
        table[d // width, d % width, z, y, k] = 1.0
    return table.reshape(NX * NC * 128, NZ * NY * slice_width)


def body(queries, passages, positive):
    rows, width = queries.shape
    cols, slice_width = passages.shape
    sub = cols // NY
    place = jnp.asarray(placement(slice_width, width), bf16)

    spare = jnp.stack([positive // 128, positive % 128], axis=1).astype(bf16)
    message = jnp.concatenate([queries, spare, jnp.zeros((rows, 126 - width), bf16)], axis=1)
    query_parts = share(message, SHORT, NY * NX * NC)
    query_full = (
        query_parts.reshape(NY, NX * NC, rows, 128).transpose(0, 2, 1, 3).reshape(NY * rows, NX * NC * 128)
    )

    part = passages.T.reshape(slice_width, NY, sub).transpose(1, 0, 2)
    part = lax.all_to_all(part, "y", 0, 0, tiled=True).reshape(NY * slice_width, sub)
    passage_part = lax.all_gather(part, "z", axis=0, tiled=True)
    passage_full = jnp.dot(place, passage_part, preferred_element_type=f32).astype(bf16)

    logit_tile = logit_scale * jnp.dot(query_full, passage_full, preferred_element_type=f32)
    row_top = jnp.max(logit_tile, axis=1)
    row_sum = jnp.sum(jnp.exp(logit_tile - row_top[:, None]), axis=1)
    col_top = jnp.max(logit_tile, axis=0)
    col_sum = jnp.sum(jnp.exp(logit_tile - col_top[None, :]), axis=0)
    col_lse = merge(share(jnp.stack([col_top, col_sum]), "z", NZ))
    row_lse = merge(share(jnp.stack([row_top, row_sum]), SHORT, NY * NX * NC))

    block = (lax.axis_index("x") * NC + lax.axis_index("core")) * NY + lax.axis_index("y")
    column_ids = (block * sub + jnp.arange(sub, dtype=jnp.int32)).astype(f32)
    target = query_full[:, width].astype(f32) * 128.0 + query_full[:, width + 1].astype(f32)
    hit = (target[:, None] == column_ids[None, :]).astype(f32)
    dlogits = (
        jnp.exp(logit_tile - row_lse[:, None]) + jnp.exp(logit_tile - col_lse[None, :]) - 2.0 * hit
    ).astype(bf16)

    query_placed = jnp.dot(query_full, place, preferred_element_type=f32).astype(bf16)
    passage_terms = logit_scale * lax.dot_general(
        query_placed, dlogits, (((0,), (0,)), ((), ())), preferred_element_type=f32
    )
    passage_terms = passage_terms.astype(bf16).reshape(NZ, NY * slice_width, sub)
    passage_terms = lax.all_to_all(passage_terms, "z", 0, 0, tiled=True)
    passage_terms = jnp.sum(passage_terms.astype(f32), axis=0).reshape(NY, slice_width, sub)
    passage_terms = lax.all_to_all(passage_terms, "y", 0, 0, tiled=True)
    passage_grad = passage_terms.transpose(1, 0, 2).reshape(slice_width, cols).T

    query_terms = logit_scale * lax.dot_general(
        dlogits, passage_full, (((1,), (1,)), ((), ())), preferred_element_type=f32
    )
    query_terms = query_terms.astype(bf16).reshape(NY, rows, NX * NC, 128).transpose(0, 2, 1, 3)
    query_terms = lax.all_to_all(query_terms.reshape(NY * NX * NC, rows, 128), SHORT, 0, 0, tiled=True)
    query_grad = jnp.sum(query_terms.astype(f32), axis=0)[:, :width]
    return (query_grad, passage_grad)


def solution(mesh):
    chips = Mesh(mesh.devices.reshape(NY, NZ, NX, NC), ("y", "z", "x", "core"))
    yz, xc = ("y", "z"), ("x", "core")
    return jax.shard_map(
        body,
        mesh=chips,
        in_specs=(P(yz, xc), P(xc, yz), P(yz)),
        out_specs=(P(yz, xc), P(xc, yz)),
        check_vma=False,
    )
```

```python
import jax
import jax.numpy as jnp
import numpy as np
from jax import lax
from jax.sharding import Mesh, PartitionSpec as P

logit_scale = 20.0
f32 = jnp.float32
bf16 = jnp.bfloat16
NY, NZ, NX, NC = 4, 16, 4, 2
SHORT = ("y", "core", "x")


def share(x, axes, n):
    return lax.all_to_all(jnp.broadcast_to(x[None], (n, *x.shape)), axes, 0, 0, tiled=True)


def merge(pairs):
    top = jnp.max(pairs[:, 0], axis=0)
    total = jnp.sum(pairs[:, 1] * jnp.exp(pairs[:, 0] - top[None]), axis=0)
    return jnp.stack([top, total])


def lse(pair):
    return pair[0] + jnp.log(pair[1])


def around(x, axis, n, step):
    return lax.ppermute(x, axis, [(i, (i + step) % n) for i in range(n)])


def pick(blocks, axis, n, step):
    return lax.dynamic_index_in_dim(blocks, (lax.axis_index(axis) + step) % n, 0, keepdims=False)


def placement(slice_width, width):
    table = np.zeros((NC, NX, 128, NZ, NY, slice_width), np.float32)
    for d in range(NX * NC * width):
        y, z, k = d // (NZ * slice_width), d // slice_width % NZ, d % slice_width
        table[d // width % NC, d // width // NC, d % width, z, y, k] = 1.0
    return table.reshape(NX * NC * 128, NZ * NY * slice_width)


def body(queries, passages, positive):
    rows, width = queries.shape
    cols, slice_width = passages.shape
    sub = cols // NY
    place = jnp.asarray(placement(slice_width, width), bf16)

    spare = jnp.stack([positive // 128, positive % 128], axis=1).astype(bf16)
    message = jnp.concatenate([queries, spare, jnp.zeros((rows, 126 - width), bf16)], axis=1)
    query_parts = share(message, SHORT, NY * NX * NC)
    query_full = query_parts.reshape(NY, NC * NX, rows, 128).transpose(0, 2, 1, 3)
    query_full = query_full.reshape(NY * rows, NC * NX * 128)

    part = passages.T.reshape(slice_width, NY, sub).transpose(1, 0, 2)
    part = lax.all_to_all(part, "y", 0, 0, tiled=True).reshape(NY * slice_width, sub)
    passage_part = lax.all_gather(part, "z", axis=0, tiled=True)
    passage_full = jnp.dot(place, passage_part, preferred_element_type=f32).astype(bf16)

    logit_tile = logit_scale * jnp.dot(query_full, passage_full, preferred_element_type=f32)
    row_top = jnp.max(logit_tile, axis=1)
    row_sum = jnp.sum(jnp.exp(logit_tile - row_top[:, None]), axis=1)
    col_top = jnp.max(logit_tile, axis=0)
    col_sum = jnp.sum(jnp.exp(logit_tile - col_top[None, :]), axis=0)
    col_lse = lse(merge(share(jnp.stack([col_top, col_sum]), "z", NZ)))
    row_pair = merge(lax.all_gather(jnp.stack([row_top, row_sum]), "core"))
    for axis, n in (("x", NX), ("y", NY)):
        row_pair = merge(jnp.stack([row_pair] + [around(row_pair, axis, n, step) for step in range(1, n)]))
    row_lse = lse(row_pair)

    block = (lax.axis_index("x") * NC + lax.axis_index("core")) * NY + lax.axis_index("y")
    column_ids = (block * sub + jnp.arange(sub, dtype=jnp.int32)).astype(f32)
    target = query_full[:, width].astype(f32) * 128.0 + query_full[:, width + 1].astype(f32)
    hit = (target[:, None] == column_ids[None, :]).astype(f32)
    dlogits = (
        jnp.exp(logit_tile - row_lse[:, None]) + jnp.exp(logit_tile - col_lse[None, :]) - 2.0 * hit
    ).astype(bf16)

    query_placed = jnp.dot(query_full, place, preferred_element_type=f32).astype(bf16)
    passage_terms = logit_scale * lax.dot_general(
        query_placed, dlogits, (((0,), (0,)), ((), ())), preferred_element_type=f32
    )
    passage_terms = passage_terms.astype(bf16).reshape(NZ, NY * slice_width, sub)
    passage_terms = lax.all_to_all(passage_terms, "z", 0, 0, tiled=True)
    passage_terms = jnp.sum(passage_terms.astype(f32), axis=0).reshape(NY, slice_width, sub)
    passage_terms = lax.all_to_all(passage_terms, "y", 0, 0, tiled=True)
    passage_grad = passage_terms.transpose(1, 0, 2).reshape(slice_width, cols).T

    halves = passage_full.reshape(NC, NX * 128, sub)
    ours, theirs = (
        logit_scale
        * lax.dot_general(
            dlogits, pick(halves, "core", NC, step), (((1,), (1,)), ((), ())), preferred_element_type=f32
        )
        for step in range(NC)
    )
    blocks = (ours + around(theirs, "core", NC, 1)).reshape(NY * rows, NX, 128).transpose(1, 0, 2)
    terms = pick(blocks, "x", NX, 0)
    for step in range(1, NX):
        terms += around(pick(blocks, "x", NX, step).astype(bf16), "x", NX, step).astype(f32)
    blocks = terms.reshape(NY, rows, 128)
    terms = pick(blocks, "y", NY, 0)
    for step in range(1, NY):
        terms += around(pick(blocks, "y", NY, step), "y", NY, step)
    query_grad = terms[:, :width]
    return (query_grad, passage_grad)


def solution(mesh):
    chips = Mesh(mesh.devices.reshape(NY, NZ, NX, NC), ("y", "z", "x", "core"))
    yz, xc = ("y", "z"), ("x", "core")
    return jax.shard_map(
        body,
        mesh=chips,
        in_specs=(P(yz, xc), P(xc, yz), P(yz)),
        out_specs=(P(yz, xc), P(xc, yz)),
        check_vma=False,
    )
```

```python
import jax
import jax.numpy as jnp
import numpy as np
from jax import lax
from jax.experimental import pallas as pl
from jax.experimental.pallas import tpu as pltpu
from jax.sharding import Mesh, PartitionSpec as P

logit_scale = 20.0
f32 = jnp.float32
bf16 = jnp.bfloat16
NY, NZ, NX, NC = 4, 16, 4, 2
ROWS, WIDTH = 144, 96
COLS, SLICE = 1152, 12
TALL, SUB = NY * ROWS, COLS // NY
HALF = NX * 128
THIRD = NZ * NY * SLICE // NC
BLOCKS = [(0, 128), (128, 128), (256, 128), (384, 128), (512, 64)]
MSG = ROWS + 48
NT = (((1,), (1,)), ((), ()))


def call(kernel, outs, *args, scratch=(), flops=0):
    bytes_accessed = sum(int(np.prod(a.shape)) * a.dtype.itemsize for a in (*args, *outs))
    vmem = pl.BlockSpec(memory_space=pltpu.VMEM)
    smem = pl.BlockSpec(memory_space=pltpu.SMEM)
    return pl.pallas_call(
        kernel,
        out_shape=outs,
        in_specs=[smem if a.ndim == 1 else vmem for a in args],
        out_specs=[vmem] * len(outs),
        scratch_shapes=list(scratch),
        compiler_params=pltpu.CompilerParams(vmem_limit_bytes=32 << 20),
        cost_estimate=pl.CostEstimate(flops=flops, bytes_accessed=bytes_accessed, transcendentals=0),
    )(*args)


def shape(dtype, *dims):
    return jax.ShapeDtypeStruct(dims, dtype)


def placement():
    table = np.zeros((NX, 128, NZ // NC, NY, SLICE), np.float32)
    for x in range(NX):
        for lane in range(WIDTH):
            table[x, lane, lane // SLICE, x, lane % SLICE] = 1.0
    return table.reshape(HALF, THIRD)


def tile_kernel(parts, passages, place, logits, row_pairs, col_pairs, query_full, passage_full):
    for y in range(NY):
        for b in range(NC * NX):
            query_full[y * ROWS : (y + 1) * ROWS, b * 128 : (b + 1) * 128] = parts[y * NC * NX + b]
    for c in range(NC):
        placed = jnp.dot(place[...], passages[c * THIRD : (c + 1) * THIRD], preferred_element_type=f32)
        passage_full[c * HALF : (c + 1) * HALF] = placed.astype(bf16)
    lane = lax.broadcasted_iota(jnp.int32, (128, 128), 1)
    packed = jnp.ones((128, 128), f32)
    col_top = None
    for j, (start, size) in enumerate(BLOCKS):
        scores = logit_scale * jnp.dot(
            query_full[start : start + size], passage_full[...], preferred_element_type=f32
        )
        logits[start : start + size] = scores
        top = jnp.max(scores, axis=1, keepdims=True)
        total = jnp.sum(jnp.exp(scores - top), axis=1, keepdims=True)
        if size < 128:
            fill = jnp.ones((128 - size, 1), f32)
            top, total = jnp.concatenate([top, fill], axis=0), jnp.concatenate([total, fill], axis=0)
        packed = jnp.where(lane == j, top, jnp.where(lane == j + 8, total, packed))
        peak = jnp.max(scores, axis=0, keepdims=True)
        col_top = peak if col_top is None else jnp.maximum(col_top, peak)
    turned = packed.T[:16]
    for i in range(NX * NC):
        row_pairs[i] = turned
    col_sum = jnp.zeros((1, SUB), f32)
    for start, size in BLOCKS:
        col_sum += jnp.sum(jnp.exp(logits[start : start + size] - col_top), axis=0, keepdims=True)
    fill = jnp.ones((1, 384 - SUB), f32)
    both = [jnp.concatenate([v, fill], axis=1) for v in (col_top, col_sum)]
    lines = [v[:, b * 128 : (b + 1) * 128] for v in both for b in range(3)]
    lines = jnp.concatenate(lines + [jnp.ones((2, 128), f32)], axis=0)
    for i in range(NZ):
        col_pairs[i] = lines


def turn_kernel(query_full, place, ids, placed, hits):
    for c in range(NC):
        half = query_full[:, c * HALF : (c + 1) * HALF]
        placed[c * THIRD : (c + 1) * THIRD] = lax.dot_general(
            place[...], half, NT, preferred_element_type=f32
        ).astype(bf16)
    spare = query_full[:, :128].astype(f32)
    target = spare[:, WIDTH : WIDTH + 1] * 128.0 + spare[:, WIDTH + 1 : WIDTH + 2]
    hits[...] = jnp.where(target == ids[...], 2.0, 0.0)


def passage_kernel(logits, hits, placed, row_pairs, col_pairs, dlogits, terms):
    top, total = row_pairs[:, :8], row_pairs[:, 8:]
    peak = jnp.max(top, axis=0)
    row_lse = peak + jnp.log(jnp.sum(total * jnp.exp(top - peak[None]), axis=0))
    row_lse = jnp.concatenate([row_lse, jnp.zeros((120, 128), f32)], axis=0).T
    pairs = col_pairs[...]
    top, total = pairs[:, 0:3], pairs[:, 3:6]
    peak = jnp.max(top, axis=0)
    col_lse = peak + jnp.log(jnp.sum(total * jnp.exp(top - peak[None]), axis=0))
    col_lse = jnp.concatenate([col_lse[b : b + 1] for b in range(3)], axis=1)[:, :SUB]
    for j, (start, size) in enumerate(BLOCKS):
        scores = logits[start : start + size]
        slope = jnp.exp(scores - row_lse[:size, j : j + 1]) + jnp.exp(scores - col_lse)
        dlogits[start : start + size] = (slope - hits[start : start + size]).astype(bf16)
    for start in range(0, NC * THIRD, 192):
        part = jnp.dot(placed[start : start + 192], dlogits[...], preferred_element_type=f32)
        terms[start : start + 192] = (logit_scale * part).astype(bf16)


def theirs_kernel(place, dlogits, passage_full, theirs):
    core = place[0]
    half = passage_full[pl.ds(pl.multiple_of((1 - core) * HALF, HALF), HALF)]
    theirs[...] = logit_scale * lax.dot_general(dlogits[...], half, NT, preferred_element_type=f32)


def ours_kernel(place, dlogits, passage_full, theirs, own, *rest):
    outs, total = rest[:-1], rest[-1]
    core, x = place[0], place[1]
    half = passage_full[pl.ds(pl.multiple_of(core * HALF, HALF), HALF)]
    total[...] = theirs[...] + logit_scale * lax.dot_general(
        dlogits[...], half, NT, preferred_element_type=f32
    )
    own[...] = total[:, pl.ds(pl.multiple_of(x * 128, 128), 128)]
    for step, out in enumerate(outs, 1):
        lanes = pl.ds(pl.multiple_of(lax.rem(x + step, NX) * 128, 128), 128)
        out[...] = total[:, lanes].astype(bf16)


def fold_kernel(terms, own, *rest):
    came, message, total = rest[:-2], rest[-2], rest[-1]
    total[:, :SUB] = jnp.sum(terms[...].astype(f32), axis=0)
    total[:, SUB:] = jnp.zeros((48, 384 - SUB), f32)
    for y in range(NY):
        rows = slice(y * ROWS, (y + 1) * ROWS)
        message[y, :ROWS] = own[rows] + sum(c[rows].astype(f32) for c in came)
        for b in range(3):
            piece = total[y * SLICE : (y + 1) * SLICE, b * 128 : (b + 1) * 128]
            message[y, ROWS + b * 16 : ROWS + b * 16 + SLICE] = piece
            message[y, ROWS + b * 16 + SLICE : ROWS + b * 16 + 16] = jnp.zeros((16 - SLICE, 128), f32)


def share(x, axes, n):
    return lax.all_to_all(jnp.broadcast_to(x[None], (n, *x.shape)), axes, 0, 0, tiled=True)


def merge(pairs):
    top, total = pairs[:, :8], pairs[:, 8:]
    peak = jnp.max(top, axis=0)
    return jnp.concatenate([peak, jnp.sum(total * jnp.exp(top - peak[None]), axis=0)])


def around(x, axis, n, step):
    return lax.ppermute(x, axis, [(i, (i + step) % n) for i in range(n)])


def body(queries, passages, positive):
    table = placement()
    place, place_t = jnp.asarray(table, bf16), jnp.asarray(table.T, bf16)
    where = jnp.stack([lax.axis_index("core"), lax.axis_index("x")]).astype(jnp.int32)

    spare = jnp.stack([positive // 128, positive % 128], axis=1).astype(bf16)
    message = jnp.concatenate([queries, spare, jnp.zeros((ROWS, 126 - WIDTH), bf16)], axis=1)
    parts = share(message, ("y", "core", "x"), NY * NC * NX)

    part = passages.T.reshape(SLICE, NY, SUB).transpose(1, 0, 2)
    part = lax.all_to_all(part, "y", 0, 0, tiled=True).reshape(NY * SLICE, SUB)
    passage_part = lax.all_gather(part, "z", axis=0, tiled=True)

    logits, row_pairs, col_pairs, query_full, passage_full = call(
        tile_kernel,
        [
            shape(f32, TALL, SUB),
            shape(f32, NX * NC, 16, 128),
            shape(f32, NZ, 8, 128),
            shape(bf16, TALL, NC * HALF),
            shape(bf16, NC * HALF, SUB),
        ],
        parts,
        passage_part,
        place,
        flops=2 * TALL * SUB * NC * HALF,
    )
    row_pairs = lax.all_to_all(row_pairs, ("x", "core"), 0, 0, tiled=True)
    col_pairs = lax.all_to_all(col_pairs, "z", 0, 0, tiled=True)
    row_pairs = lax.all_gather(merge(row_pairs), "y")

    block = (lax.axis_index("x") * NC + lax.axis_index("core")) * NY + lax.axis_index("y")
    ids = (block * SUB + jnp.arange(SUB, dtype=jnp.int32)).astype(f32)[None]
    placed, hits = call(
        turn_kernel,
        [shape(bf16, NC * THIRD, TALL), shape(f32, TALL, SUB)],
        query_full,
        place_t,
        ids,
        flops=2 * TALL * HALF * THIRD * NC,
    )
    dlogits, terms = call(
        passage_kernel,
        [shape(bf16, TALL, SUB), shape(bf16, NC * THIRD, SUB)],
        logits,
        hits,
        placed,
        row_pairs,
        col_pairs,
        flops=2 * TALL * SUB * NC * THIRD,
    )
    terms = lax.all_to_all(terms.reshape(NZ, NY * SLICE, SUB), "z", 0, 0, tiled=True)

    (theirs,) = call(
        theirs_kernel, [shape(f32, TALL, HALF)], where, dlogits, passage_full, flops=2 * TALL * SUB * HALF
    )
    theirs = around(theirs, "core", NC, 1)
    own, *others = call(
        ours_kernel,
        [shape(f32, TALL, 128)] + [shape(bf16, TALL, 128)] * (NX - 1),
        where,
        dlogits,
        passage_full,
        theirs,
        scratch=[pltpu.VMEM((TALL, HALF), f32)],
        flops=2 * TALL * SUB * HALF,
    )
    came = [around(other, "x", NX, step) for step, other in enumerate(others, 1)]

    (message,) = call(fold_kernel, [shape(f32, NY, MSG, 128)], terms, own, *came, scratch=[pltpu.VMEM((48, 384), f32)])
    message = lax.all_to_all(message, "y", 0, 0, tiled=True)
    query_grad = jnp.sum(message[:, :ROWS, :WIDTH], axis=0)
    blocks = message[:, ROWS:].reshape(NY, 3, 16, 128)[:, :, :SLICE].transpose(2, 0, 1, 3)
    passage_grad = blocks.reshape(SLICE, NY, 384)[:, :, :SUB].reshape(SLICE, COLS).T
    return (query_grad, passage_grad)


def solution(mesh):
    chips = Mesh(mesh.devices.reshape(NY, NZ, NX, NC), ("y", "z", "x", "core"))
    yz, xc = ("y", "z"), ("x", "core")
    return jax.shard_map(
        body,
        mesh=chips,
        in_specs=(P(yz, xc), P(xc, yz), P(yz)),
        out_specs=(P(yz, xc), P(xc, yz)),
        check_vma=False,
    )
```

```python
import jax
import jax.numpy as jnp
import numpy as np
from jax import lax
from jax.experimental import pallas as pl
from jax.experimental.pallas import tpu as pltpu
from jax.sharding import Mesh, PartitionSpec as P

logit_scale = 20.0
f32 = jnp.float32
bf16 = jnp.bfloat16
NY, NZ, NX, NC = 4, 16, 4, 2
ROWS, WIDTH = 144, 96
COLS, SLICE = 1152, 12
TALL, SUB = NY * ROWS, COLS // NY
HALF = NX * 128
THIRD = NZ * NY * SLICE // NC
BLOCKS = [(0, 128), (128, 128), (256, 128), (384, 128), (512, 64)]
MSG = ROWS + 48
NT = (((1,), (1,)), ((), ()))


def call(kernel, outs, *args, far=(), far_outs=(), scratch=(), flops=0):
    bytes_accessed = sum(int(np.prod(a.shape)) * a.dtype.itemsize for a in (*args, *outs))
    vmem, smem, hbm = (pl.BlockSpec(memory_space=m) for m in (pltpu.VMEM, pltpu.SMEM, pltpu.HBM))
    return pl.pallas_call(
        kernel,
        out_shape=outs,
        in_specs=[hbm if i in far else smem if a.ndim == 1 else vmem for i, a in enumerate(args)],
        out_specs=[hbm if i in far_outs else vmem for i in range(len(outs))],
        scratch_shapes=list(scratch),
        compiler_params=pltpu.CompilerParams(vmem_limit_bytes=32 << 20),
        cost_estimate=pl.CostEstimate(flops=flops, bytes_accessed=bytes_accessed, transcendentals=0),
    )(*args)


def shape(dtype, *dims):
    return jax.ShapeDtypeStruct(dims, dtype)


def placement():
    table = np.zeros((NX, 128, NZ // NC, NY, SLICE), np.float32)
    for x in range(NX):
        for lane in range(WIDTH):
            table[x, lane, lane // SLICE, x, lane % SLICE] = 1.0
    return table.reshape(HALF, THIRD)


def columns(wide, width):
    lane = lax.broadcasted_iota(jnp.int32, (128, 128), 1)
    packed = jnp.ones((128, 128), f32)
    for j, group in enumerate(wide):
        for g, column in enumerate(group):
            if column.shape[0] < 128:
                column = jnp.concatenate([column, jnp.ones((128 - column.shape[0], 1), f32)], axis=0)
            packed = jnp.where(lane == 8 * g + j, column, packed)
    return packed.T[:width]


def upright(lines):
    return jnp.concatenate([lines, jnp.zeros((120, 128), f32)], axis=0).T


def prep_kernel(queries, positive, passages, message, wide, tall):
    index = positive[...].astype(f32)
    index = jnp.concatenate(
        [index[:, :128], jnp.concatenate([index[:, 128:], jnp.zeros((1, 256 - ROWS), f32)], axis=1)], axis=0
    )
    index = upright(jnp.concatenate([index, jnp.zeros((6, 128), f32)], axis=0))
    index = jnp.concatenate([index[:, 0:1], index[: ROWS - 128, 1:2]], axis=0)
    high = jnp.floor(index * (1.0 / 128.0))
    low = index - 128.0 * high
    wide[...] = jnp.zeros((ROWS, 128), f32)
    wide[:, :WIDTH] = queries[...].astype(f32)
    lane = lax.broadcasted_iota(jnp.int32, (ROWS, 128), 1)
    own = jnp.where(lane == WIDTH, high, jnp.where(lane == WIDTH + 1, low, wide[...])).astype(bf16)
    tall[...] = jnp.zeros((16, COLS), f32)
    tall[:SLICE] = passages[...].astype(f32)
    for y in range(NY):
        message[y, :ROWS] = own
        piece = pltpu.roll(tall[...], (COLS - y * SUB) % COLS, 1)
        for b in range(3):
            message[y, ROWS + 16 * b : ROWS + 16 * b + 16] = piece[:, b * 128 : (b + 1) * 128].astype(bf16)


def split_kernel(came, queries, part, total):
    for y in range(NY):
        for b in range(3):
            piece = came[y, ROWS + 16 * b : ROWS + 16 * b + 16].astype(f32)
            total[y * SLICE : (y + 1) * SLICE, b * 128 : (b + 1) * 128] = piece[:SLICE]
        for i in range(NX * NC):
            queries[i, y * ROWS : (y + 1) * ROWS] = came[y, :ROWS]
    part[...] = total[:, :SUB].astype(bf16)


def gather_parts(parts, query_full, sems):
    copies = [
        pltpu.make_async_copy(parts.at[b], query_full.at[:, pl.ds(b * 128, 128)], sems.at[b])
        for b in range(NC * NX)
    ]
    for copy in copies:
        copy.start()
    return copies


def tile_kernel(parts, passages, place, logits, row_pairs, col_pairs, passage_full, query_full, kept, sems, out_sems):
    copies = gather_parts(parts, query_full, sems)
    for c in range(NC):
        placed = jnp.dot(place[...], passages[c * THIRD : (c + 1) * THIRD], preferred_element_type=f32)
        passage_full[c * HALF : (c + 1) * HALF] = placed.astype(bf16)
    for copy in copies:
        copy.wait()
    pairs, col_top, out = [], None, []
    for j, (start, size) in enumerate(BLOCKS):
        rows = pl.ds(start, size)
        scores = logit_scale * jnp.dot(query_full[rows], passage_full[...], preferred_element_type=f32)
        kept[rows] = scores
        out.append(pltpu.make_async_copy(kept.at[rows], logits.at[rows], out_sems.at[j]))
        out[-1].start()
        top = jnp.max(scores, axis=1, keepdims=True)
        pairs.append((top, jnp.sum(jnp.exp(scores - top), axis=1, keepdims=True)))
        peak = jnp.max(scores, axis=0, keepdims=True)
        col_top = peak if col_top is None else jnp.maximum(col_top, peak)
    turned = columns(pairs, 16)
    for i in range(NX * NC):
        row_pairs[i] = turned
    col_sum = jnp.zeros((1, SUB), f32)
    for start, size in BLOCKS:
        col_sum += jnp.sum(jnp.exp(kept[start : start + size] - col_top), axis=0, keepdims=True)
    fill = jnp.ones((1, 384 - SUB), f32)
    both = [jnp.concatenate([v, fill], axis=1) for v in (col_top, col_sum)]
    lines = [v[:, b * 128 : (b + 1) * 128] for v in both for b in range(3)]
    lines = jnp.concatenate(lines + [jnp.ones((2, 128), f32)], axis=0)
    for i in range(NZ):
        col_pairs[i] = lines
    for copy in out:
        copy.wait()


def turn_kernel(parts, place, placed, targets, query_full, sems):
    for copy in gather_parts(parts, query_full, sems):
        copy.wait()
    for c in range(NC):
        half = query_full[:, c * HALF : (c + 1) * HALF]
        placed[c * THIRD : (c + 1) * THIRD] = lax.dot_general(
            place[...], half, NT, preferred_element_type=f32
        ).astype(bf16)
    spare = query_full[:, :128].astype(f32)
    target = spare[:, WIDTH : WIDTH + 1] * 128.0 + spare[:, WIDTH + 1 : WIDTH + 2]
    targets[...] = columns([(target[start : start + size],) for start, size in BLOCKS], 8)


def passage_kernel(
    logits, targets, ids, placed, row_pairs, col_pairs, dlogits, terms, kept, tails, sems
):
    copies = [
        pltpu.make_async_copy(logits.at[pl.ds(start, size)], kept.at[pl.ds(start, size)], sems.at[j])
        for j, (start, size) in enumerate(BLOCKS)
    ]
    for copy in copies:
        copy.start()
    top, total = row_pairs[:, :8], row_pairs[:, 8:]
    peak = jnp.max(top, axis=0)
    row_lse = upright(peak + jnp.log(jnp.sum(total * jnp.exp(top - peak[None]), axis=0)))
    target = upright(targets[...])
    pairs = col_pairs[...]
    top, total = pairs[:, 0:3], pairs[:, 3:6]
    peak = jnp.max(top, axis=0)
    col_lse = peak + jnp.log(jnp.sum(total * jnp.exp(top - peak[None]), axis=0))
    col_lse = jnp.concatenate([col_lse[b : b + 1] for b in range(3)], axis=1)[:, :SUB]
    dlogits[:, 256:] = jnp.zeros((TALL, 128), bf16)
    for j, (start, size) in enumerate(BLOCKS):
        copies[j].wait()
        scores = kept[start : start + size]
        slope = jnp.exp(scores - row_lse[:size, j : j + 1]) + jnp.exp(scores - col_lse)
        hit = jnp.where(target[:size, j : j + 1] == ids[...], 2.0, 0.0)
        dlogits[start : start + size, :SUB] = (slope - hit).astype(bf16)
    high = NY * SLICE
    for first in range(0, NZ, 4):
        part = logit_scale * jnp.dot(
            placed[first * high : (first + 4) * high], dlogits[...], preferred_element_type=f32
        )
        for a in range(NY):
            tails[a] = part[:, 256:] if a == 0 else pltpu.roll(part[:, 256:], 32 * a, 1)
        for i in range(4):
            for b in range(2):
                piece = part[i * high : (i + 1) * high, b * 128 : (b + 1) * 128]
                terms[first + i, b * high : (b + 1) * high] = piece.astype(bf16)
            tail = sum(tails[a, i * high + a * SLICE : i * high + (a + 1) * SLICE] for a in range(NY))
            tail = jnp.concatenate([tail, jnp.zeros((16 - SLICE, 128), f32)], axis=0)
            terms[first + i, 2 * high : 2 * high + 16] = tail.astype(bf16)


def theirs_kernel(place, dlogits, passage_full, theirs):
    core = place[0]
    half = passage_full[pl.ds(pl.multiple_of((1 - core) * HALF, HALF), HALF)]
    theirs[...] = logit_scale * lax.dot_general(dlogits[:, :SUB], half, NT, preferred_element_type=f32)


def ours_kernel(place, dlogits, passage_full, theirs, own, *rest):
    outs, total = rest[:-1], rest[-1]
    core, x = place[0], place[1]
    half = passage_full[pl.ds(pl.multiple_of(core * HALF, HALF), HALF)]
    total[...] = theirs[...] + logit_scale * lax.dot_general(
        dlogits[:, :SUB], half, NT, preferred_element_type=f32
    )
    own[...] = total[:, pl.ds(pl.multiple_of(x * 128, 128), 128)]
    for step, out in enumerate(outs, 1):
        lanes = pl.ds(pl.multiple_of(lax.rem(x + step, NX) * 128, 128), 128)
        out[...] = total[:, lanes].astype(bf16)


def fold_kernel(terms, own, *rest):
    came, message, total = rest[:-2], rest[-2], rest[-1]
    high = NY * SLICE
    total[...] = jnp.sum(terms[...].astype(f32), axis=0)
    for y in range(NY):
        rows = slice(y * ROWS, (y + 1) * ROWS)
        message[y, :ROWS] = own[rows] + sum(c[rows].astype(f32) for c in came)
        tail = total[2 * high :]
        tail = tail if y == 0 else pltpu.roll(tail, 128 - 32 * y, 1)
        for b in range(3):
            piece = tail[:SLICE] if b == 2 else total[b * high + y * SLICE : b * high + (y + 1) * SLICE]
            message[y, ROWS + b * 16 : ROWS + b * 16 + SLICE] = piece
            message[y, ROWS + b * 16 + SLICE : ROWS + b * 16 + 16] = jnp.zeros((16 - SLICE, 128), f32)


def final_kernel(came, query_grad, passage_grad):
    query_grad[...] = jnp.sum(came[:, :ROWS], axis=0)[:, :WIDTH]
    lane = lax.broadcasted_iota(jnp.int32, (16, 128), 1)
    total = None
    for y in range(NY):
        blocks = [came[y, ROWS + b * 16 : ROWS + b * 16 + 16] for b in range(3)]
        blocks[2] = jnp.where(lane < SUB - 256, blocks[2], 0.0)
        wide = jnp.concatenate(blocks + [jnp.zeros((16, COLS - 384), f32)], axis=1)
        wide = wide if y == 0 else pltpu.roll(wide, y * SUB, 1)
        total = wide if total is None else total + wide
    passage_grad[...] = total[:SLICE]


def merge(pairs):
    top, total = pairs[:, :8], pairs[:, 8:]
    peak = jnp.max(top, axis=0)
    return jnp.concatenate([peak, jnp.sum(total * jnp.exp(top - peak[None]), axis=0)])


def around(x, axis, n, step):
    return lax.ppermute(x, axis, [(i, (i + step) % n) for i in range(n)])


def body(queries, passages, positive):
    table = placement()
    place, place_t = jnp.asarray(table, bf16), jnp.asarray(table.T, bf16)
    where = jnp.stack([lax.axis_index("core"), lax.axis_index("x")]).astype(jnp.int32)

    (message,) = call(
        prep_kernel,
        [shape(bf16, NY, MSG, 128)],
        queries,
        positive[None],
        passages.T,
        scratch=[pltpu.VMEM((ROWS, 128), f32), pltpu.VMEM((16, COLS), f32)],
    )
    message = lax.all_to_all(message, "y", 0, 0, tiled=True)
    parts, passage_part = call(
        split_kernel,
        [shape(bf16, NX * NC, TALL, 128), shape(bf16, NY * SLICE, SUB)],
        message,
        scratch=[pltpu.VMEM((NY * SLICE, 384), f32)],
    )
    parts = lax.all_to_all(parts, ("core", "x"), 0, 0, tiled=True)
    passage_part = lax.all_gather(passage_part, "z", axis=0, tiled=True)

    assembly = [pltpu.VMEM((TALL, NC * HALF), bf16), pltpu.SemaphoreType.DMA((NC * NX,))]
    kept = pltpu.VMEM((TALL, SUB), f32)
    logits, row_pairs, col_pairs, passage_full = call(
        tile_kernel,
        [
            shape(f32, TALL, SUB),
            shape(f32, NX * NC, 16, 128),
            shape(f32, NZ, 8, 128),
            shape(bf16, NC * HALF, SUB),
        ],
        parts,
        passage_part,
        place,
        far=(0,),
        far_outs=(0,),
        scratch=[assembly[0], kept, assembly[1], pltpu.SemaphoreType.DMA((len(BLOCKS),))],
        flops=2 * TALL * SUB * NC * HALF,
    )
    placed, targets = call(
        turn_kernel,
        [shape(bf16, NC * THIRD, TALL), shape(f32, 8, 128)],
        parts,
        place_t,
        far=(0,),
        scratch=assembly,
        flops=2 * TALL * HALF * THIRD * NC,
    )
    row_pairs = lax.all_to_all(row_pairs, ("x", "core"), 0, 0, tiled=True)
    col_pairs = lax.all_to_all(col_pairs, "z", 0, 0, tiled=True)
    row_pairs = lax.all_gather(merge(row_pairs), "y")

    block = (lax.axis_index("x") * NC + lax.axis_index("core")) * NY + lax.axis_index("y")
    ids = (block * SUB + jnp.arange(SUB, dtype=jnp.int32)).astype(f32)[None]
    dlogits, terms = call(
        passage_kernel,
        [shape(bf16, TALL, 384), shape(bf16, NZ, 112, 128)],
        logits,
        targets,
        ids,
        placed,
        row_pairs,
        col_pairs,
        far=(0,),
        scratch=[kept, pltpu.VMEM((NY, 4 * NY * SLICE, 128), f32), pltpu.SemaphoreType.DMA((len(BLOCKS),))],
        flops=2 * TALL * SUB * NC * THIRD,
    )
    terms = lax.all_to_all(terms, "z", 0, 0, tiled=True)

    (theirs,) = call(
        theirs_kernel, [shape(f32, TALL, HALF)], where, dlogits, passage_full, flops=2 * TALL * SUB * HALF
    )
    theirs = around(theirs, "core", NC, 1)
    own, *others = call(
        ours_kernel,
        [shape(f32, TALL, 128)] + [shape(bf16, TALL, 128)] * (NX - 1),
        where,
        dlogits,
        passage_full,
        theirs,
        scratch=[pltpu.VMEM((TALL, HALF), f32)],
        flops=2 * TALL * SUB * HALF,
    )
    came = [around(other, "x", NX, step) for step, other in enumerate(others, 1)]

    (message,) = call(fold_kernel, [shape(f32, NY, MSG, 128)], terms, own, *came, scratch=[pltpu.VMEM((112, 128), f32)])
    message = lax.all_to_all(message, "y", 0, 0, tiled=True)
    query_grad, passage_grad = call(final_kernel, [shape(f32, ROWS, WIDTH), shape(f32, SLICE, COLS)], message)
    return (query_grad, passage_grad.T)


def solution(mesh):
    chips = Mesh(mesh.devices.reshape(NY, NZ, NX, NC), ("y", "z", "x", "core"))
    yz, xc = ("y", "z"), ("x", "core")
    return jax.shard_map(
        body,
        mesh=chips,
        in_specs=(P(yz, xc), P(xc, yz), P(yz)),
        out_specs=(P(yz, xc), P(xc, yz)),
        check_vma=False,
    )
```

```python
import jax
import jax.numpy as jnp
import numpy as np
from jax import lax
from jax.experimental import pallas as pl
from jax.experimental.pallas import tpu as pltpu
from jax.sharding import Mesh, PartitionSpec as P

logit_scale = 20.0
f32 = jnp.float32
bf16 = jnp.bfloat16
NY, NZ, NX, NC = 4, 16, 4, 2
ROWS, WIDTH = 144, 96
COLS, SLICE = 1152, 12
TALL, SUB = NY * ROWS, COLS // NY
HALF = NX * 128
THIRD = NZ * NY * SLICE // NC
BLOCKS = [(0, 128), (128, 128), (256, 128), (384, 128), (512, 64)]
MSG = ROWS + 48
GROUP = 384
NT = (((1,), (1,)), ((), ()))
TN = (((0,), (0,)), ((), ()))


def call(kernel, outs, *args, far=(), scratch=(), flops=0):
    bytes_accessed = sum(int(np.prod(a.shape)) * a.dtype.itemsize for a in (*args, *outs))
    vmem, smem, hbm = (pl.BlockSpec(memory_space=m) for m in (pltpu.VMEM, pltpu.SMEM, pltpu.HBM))
    return pl.pallas_call(
        kernel,
        out_shape=outs,
        in_specs=[hbm if i in far else smem if a.ndim == 1 else vmem for i, a in enumerate(args)],
        out_specs=[vmem] * len(outs),
        scratch_shapes=list(scratch),
        compiler_params=pltpu.CompilerParams(vmem_limit_bytes=32 << 20),
        cost_estimate=pl.CostEstimate(flops=flops, bytes_accessed=bytes_accessed, transcendentals=0),
    )(*(pltpu.with_memory_space_constraint(a, pltpu.HBM) if i in far else a for i, a in enumerate(args)))


def shape(dtype, *dims):
    return jax.ShapeDtypeStruct(dims, dtype)


def placement():
    table = np.zeros((NX, 128, NZ // NC, NY, SLICE), np.float32)
    for x in range(NX):
        for lane in range(WIDTH):
            table[x, lane, lane // SLICE, x, lane % SLICE] = 1.0
    return table.reshape(HALF, THIRD)


def columns(wide, width):
    lane = lax.broadcasted_iota(jnp.int32, (128, 128), 1)
    packed = jnp.ones((128, 128), f32)
    for j, group in enumerate(wide):
        for g, column in enumerate(group):
            if column.shape[0] < 128:
                column = jnp.concatenate([column, jnp.ones((128 - column.shape[0], 1), f32)], axis=0)
            packed = jnp.where(lane == 8 * g + j, column, packed)
    return packed.T[:width]


def upright(lines):
    return jnp.concatenate([lines, jnp.zeros((120, 128), f32)], axis=0).T


def prep_kernel(queries_in, positive_in, passages_in, message, queries, positive, passages, wide, tall, sems):
    pairs = ((queries_in, queries), (positive_in, positive), (passages_in, passages))
    copies = [pltpu.make_async_copy(a, b, sems.at[i]) for i, (a, b) in enumerate(pairs)]
    for copy in copies:
        copy.start()
    for copy in copies:
        copy.wait()
    index = positive[...].astype(f32)
    index = jnp.concatenate(
        [index[:, :128], jnp.concatenate([index[:, 128:], jnp.zeros((1, 256 - ROWS), f32)], axis=1)], axis=0
    )
    index = upright(jnp.concatenate([index, jnp.zeros((6, 128), f32)], axis=0))
    index = jnp.concatenate([index[:, 0:1], index[: ROWS - 128, 1:2]], axis=0)
    high = jnp.floor(index * (1.0 / 128.0))
    low = index - 128.0 * high
    wide[...] = jnp.zeros((ROWS, 128), f32)
    wide[:, :WIDTH] = queries[...].astype(f32)
    lane = lax.broadcasted_iota(jnp.int32, (ROWS, 128), 1)
    own = jnp.where(lane == WIDTH, high, jnp.where(lane == WIDTH + 1, low, wide[...])).astype(bf16)
    tall[...] = jnp.zeros((16, COLS), f32)
    tall[:SLICE] = passages[...].astype(f32)
    for y in range(NY):
        message[y, :ROWS] = own
        piece = pltpu.roll(tall[...], (COLS - y * SUB) % COLS, 1)
        for b in range(3):
            message[y, ROWS + 16 * b : ROWS + 16 * b + 16] = piece[:, b * 128 : (b + 1) * 128].astype(bf16)


def split_kernel(came, queries, part, total):
    for y in range(NY):
        for b in range(3):
            piece = came[y, ROWS + 16 * b : ROWS + 16 * b + 16].astype(f32)
            total[y * SLICE : (y + 1) * SLICE, b * 128 : (b + 1) * 128] = piece[:SLICE]
        for i in range(NX * NC):
            queries[i, y * ROWS : (y + 1) * ROWS] = came[y, :ROWS]
    part[...] = total[:, :SUB].astype(bf16)


def tile_kernel(parts, passages, place, row_pairs, col_pairs, placed, targets, query_half, logits):
    for c in range(NC):
        for x in range(NX):
            query_half[:, x * 128 : (x + 1) * 128] = parts[c * NX + x]
        placed[:, c * THIRD : (c + 1) * THIRD] = jnp.dot(
            query_half[...], place[...], preferred_element_type=f32
        ).astype(bf16)
    pairs, col_top = [], None
    for start, size in BLOCKS:
        scores = logit_scale * jnp.dot(
            placed[start : start + size], passages[...], preferred_element_type=f32
        )
        logits[start : start + size] = scores
        top = jnp.max(scores, axis=1, keepdims=True)
        pairs.append((top, jnp.sum(jnp.exp(scores - top), axis=1, keepdims=True)))
        peak = jnp.max(scores, axis=0, keepdims=True)
        col_top = peak if col_top is None else jnp.maximum(col_top, peak)
    turned = columns(pairs, 16)
    for i in range(NX * NC):
        row_pairs[i] = turned
    col_sum = jnp.zeros((1, SUB), f32)
    for start, size in BLOCKS:
        col_sum += jnp.sum(jnp.exp(logits[start : start + size] - col_top), axis=0, keepdims=True)
    fill = jnp.ones((1, 384 - SUB), f32)
    both = [jnp.concatenate([v, fill], axis=1) for v in (col_top, col_sum)]
    lines = [v[:, b * 128 : (b + 1) * 128] for v in both for b in range(3)]
    lines = jnp.concatenate(lines + [jnp.ones((2, 128), f32)], axis=0)
    for i in range(NZ):
        col_pairs[i] = lines
    spare = parts[0].astype(f32)
    target = spare[:, WIDTH : WIDTH + 1] * 128.0 + spare[:, WIDTH + 1 : WIDTH + 2]
    targets[...] = columns([(target[start : start + size],) for start, size in BLOCKS], 8)


def spread_kernel(passages, place, passage_full):
    for c in range(NC):
        turned = jnp.dot(place[...], passages[c * THIRD : (c + 1) * THIRD], preferred_element_type=f32)
        passage_full[c * HALF : (c + 1) * HALF] = turned.astype(bf16)


def passage_kernel(placed, passages, targets, ids, row_pairs, col_pairs, dlogits, terms, tails):
    top, total = row_pairs[:, :8], row_pairs[:, 8:]
    peak = jnp.max(top, axis=0)
    row_lse = upright(peak + jnp.log(jnp.sum(total * jnp.exp(top - peak[None]), axis=0)))
    target = upright(targets[...])
    pairs = col_pairs[...]
    top, total = pairs[:, 0:3], pairs[:, 3:6]
    peak = jnp.max(top, axis=0)
    col_lse = peak + jnp.log(jnp.sum(total * jnp.exp(top - peak[None]), axis=0))
    col_lse = jnp.concatenate([col_lse[b : b + 1] for b in range(3)], axis=1)[:, :SUB]
    dlogits[:, 256:] = jnp.zeros((TALL, 128), bf16)
    for j, (start, size) in enumerate(BLOCKS):
        scores = logit_scale * jnp.dot(placed[start : start + size], passages[...], preferred_element_type=f32)
        slope = jnp.exp(scores - row_lse[:size, j : j + 1]) + jnp.exp(scores - col_lse)
        hit = jnp.where(target[:size, j : j + 1] == ids[...], 2.0, 0.0)
        dlogits[start : start + size, :SUB] = (slope - hit).astype(bf16)
    high = NY * SLICE
    for first in range(0, NZ, 4):
        if first * high % GROUP == 0:
            whole = logit_scale * lax.dot_general(
                placed[:, first * high : first * high + GROUP], dlogits[...], TN, preferred_element_type=f32
            )
        offset = first * high % GROUP
        part = whole[offset : offset + 4 * high]
        for a in range(NY):
            tails[a] = part[:, 256:] if a == 0 else pltpu.roll(part[:, 256:], 32 * a, 1)
        for i in range(4):
            for b in range(2):
                piece = part[i * high : (i + 1) * high, b * 128 : (b + 1) * 128]
                terms[first + i, b * high : (b + 1) * high] = piece.astype(bf16)
            tail = sum(tails[a, i * high + a * SLICE : i * high + (a + 1) * SLICE] for a in range(NY))
            tail = jnp.concatenate([tail, jnp.zeros((16 - SLICE, 128), f32)], axis=0)
            terms[first + i, 2 * high : 2 * high + 16] = tail.astype(bf16)


def theirs_kernel(place, dlogits, passage_full, theirs):
    core = place[0]
    half = passage_full[pl.ds(pl.multiple_of((1 - core) * HALF, HALF), HALF)]
    theirs[...] = logit_scale * lax.dot_general(dlogits[:, :SUB], half, NT, preferred_element_type=f32)


def ours_kernel(place, dlogits, passage_full, theirs, own, *rest):
    outs, total = rest[:-1], rest[-1]
    core, x = place[0], place[1]
    half = passage_full[pl.ds(pl.multiple_of(core * HALF, HALF), HALF)]
    total[...] = theirs[...] + logit_scale * lax.dot_general(
        dlogits[:, :SUB], half, NT, preferred_element_type=f32
    )
    own[...] = total[:, pl.ds(pl.multiple_of(x * 128, 128), 128)]
    for step, out in enumerate(outs, 1):
        lanes = pl.ds(pl.multiple_of(lax.rem(x + step, NX) * 128, 128), 128)
        out[...] = total[:, lanes].astype(bf16)


def fold_kernel(terms, own, *rest):
    came, message, total = rest[:-2], rest[-2], rest[-1]
    high = NY * SLICE
    total[...] = jnp.sum(terms[...].astype(f32), axis=0)
    for y in range(NY):
        rows = slice(y * ROWS, (y + 1) * ROWS)
        message[y, :ROWS] = own[rows] + sum(c[rows].astype(f32) for c in came)
        tail = total[2 * high :]
        tail = tail if y == 0 else pltpu.roll(tail, 128 - 32 * y, 1)
        for b in range(3):
            piece = tail[:SLICE] if b == 2 else total[b * high + y * SLICE : b * high + (y + 1) * SLICE]
            message[y, ROWS + b * 16 : ROWS + b * 16 + SLICE] = piece
            message[y, ROWS + b * 16 + SLICE : ROWS + b * 16 + 16] = jnp.zeros((16 - SLICE, 128), f32)


def final_kernel(came, query_grad, passage_grad):
    query_grad[...] = jnp.sum(came[:, :ROWS], axis=0)[:, :WIDTH]
    lane = lax.broadcasted_iota(jnp.int32, (16, 128), 1)
    total = None
    for y in range(NY):
        blocks = [came[y, ROWS + b * 16 : ROWS + b * 16 + 16] for b in range(3)]
        blocks[2] = jnp.where(lane < SUB - 256, blocks[2], 0.0)
        wide = jnp.concatenate(blocks + [jnp.zeros((16, COLS - 384), f32)], axis=1)
        wide = wide if y == 0 else pltpu.roll(wide, y * SUB, 1)
        total = wide if total is None else total + wide
    passage_grad[...] = total[:SLICE]


def merge(pairs):
    top, total = pairs[:, :8], pairs[:, 8:]
    peak = jnp.max(top, axis=0)
    return jnp.concatenate([peak, jnp.sum(total * jnp.exp(top - peak[None]), axis=0)])


def around(x, axis, n, step):
    return lax.ppermute(x, axis, [(i, (i + step) % n) for i in range(n)])


def body(queries, passages, positive):
    place = jnp.asarray(placement(), bf16)
    where = jnp.stack([lax.axis_index("core"), lax.axis_index("x")]).astype(jnp.int32)

    (message,) = call(
        prep_kernel,
        [shape(bf16, NY, MSG, 128)],
        queries,
        positive[None],
        passages.T,
        far=(0, 1, 2),
        scratch=[
            pltpu.VMEM((ROWS, WIDTH), bf16),
            pltpu.VMEM((1, ROWS), jnp.int32),
            pltpu.VMEM((SLICE, COLS), bf16),
            pltpu.VMEM((ROWS, 128), f32),
            pltpu.VMEM((16, COLS), f32),
            pltpu.SemaphoreType.DMA((3,)),
        ],
    )
    message = lax.all_to_all(message, "y", 0, 0, tiled=True)
    parts, passage_part = call(
        split_kernel,
        [shape(bf16, NX * NC, TALL, 128), shape(bf16, NY * SLICE, SUB)],
        message,
        scratch=[pltpu.VMEM((NY * SLICE, 384), f32)],
    )
    parts = lax.all_to_all(parts, ("core", "x"), 0, 0, tiled=True)
    passage_part = lax.all_gather(passage_part, "z", axis=0, tiled=True)

    row_pairs, col_pairs, placed, targets = call(
        tile_kernel,
        [
            shape(f32, NX * NC, 16, 128),
            shape(f32, NZ, 8, 128),
            shape(bf16, TALL, NC * THIRD),
            shape(f32, 8, 128),
        ],
        parts,
        passage_part,
        place,
        scratch=[pltpu.VMEM((TALL, HALF), bf16), pltpu.VMEM((TALL, SUB), f32)],
        flops=2 * TALL * SUB * NC * HALF,
    )
    passage_part, targets = lax.optimization_barrier((passage_part, targets))
    (passage_full,) = call(
        spread_kernel,
        [shape(bf16, NC * HALF, SUB)],
        passage_part,
        place,
        flops=2 * NC * HALF * THIRD * SUB,
    )
    col_pairs, passage_full = lax.optimization_barrier((col_pairs, passage_full))
    row_pairs = lax.all_to_all(row_pairs, ("x", "core"), 0, 0, tiled=True)
    col_pairs = lax.all_to_all(col_pairs, "z", 0, 0, tiled=True)
    row_pairs = lax.all_gather(merge(row_pairs), "y")

    block = (lax.axis_index("x") * NC + lax.axis_index("core")) * NY + lax.axis_index("y")
    ids = (block * SUB + jnp.arange(SUB, dtype=jnp.int32)).astype(f32)[None]
    dlogits, terms = call(
        passage_kernel,
        [shape(bf16, TALL, 384), shape(bf16, NZ, 112, 128)],
        placed,
        passage_part,
        targets,
        ids,
        row_pairs,
        col_pairs,
        scratch=[pltpu.VMEM((NY, 4 * NY * SLICE, 128), f32)],
        flops=2 * TALL * SUB * NC * THIRD,
    )
    terms = lax.all_to_all(terms, "z", 0, 0, tiled=True)

    (theirs,) = call(
        theirs_kernel, [shape(f32, TALL, HALF)], where, dlogits, passage_full, flops=2 * TALL * SUB * HALF
    )
    theirs = around(theirs, "core", NC, 1)
    own, *others = call(
        ours_kernel,
        [shape(f32, TALL, 128)] + [shape(bf16, TALL, 128)] * (NX - 1),
        where,
        dlogits,
        passage_full,
        theirs,
        scratch=[pltpu.VMEM((TALL, HALF), f32)],
        flops=2 * TALL * SUB * HALF,
    )
    came = [around(other, "x", NX, step) for step, other in enumerate(others, 1)]

    (message,) = call(fold_kernel, [shape(f32, NY, MSG, 128)], terms, own, *came, scratch=[pltpu.VMEM((112, 128), f32)])
    message = lax.all_to_all(message, "y", 0, 0, tiled=True)
    query_grad, passage_grad = call(final_kernel, [shape(f32, ROWS, WIDTH), shape(f32, SLICE, COLS)], message)
    return (query_grad, passage_grad.T)


def solution(mesh):
    chips = Mesh(mesh.devices.reshape(NY, NZ, NX, NC), ("y", "z", "x", "core"))
    yz, xc = ("y", "z"), ("x", "core")
    return jax.shard_map(
        body,
        mesh=chips,
        in_specs=(P(yz, xc), P(xc, yz), P(yz)),
        out_specs=(P(yz, xc), P(xc, yz)),
        check_vma=False,
    )
```

```python
import jax
import jax.numpy as jnp
import numpy as np
from jax import lax
from jax.experimental import pallas as pl
from jax.experimental.pallas import tpu as pltpu
from jax.sharding import Mesh, PartitionSpec as P

logit_scale = 20.0
f32 = jnp.float32
bf16 = jnp.bfloat16
NY, NZ, NX, NC = 4, 16, 4, 2
ROWS, WIDTH = 144, 96
COLS, SLICE = 1152, 12
TALL, SUB = NY * ROWS, COLS // NY
HALF = NX * 128
THIRD = NZ * NY * SLICE // NC
BLOCKS = [(0, 128), (128, 128), (256, 128), (384, 128), (512, 64)]
MSG = ROWS + 48
GROUP = 384
NT = (((1,), (1,)), ((), ()))
TN = (((0,), (0,)), ((), ()))


def call(kernel, outs, *args, far=(), scratch=(), flops=0):
    bytes_accessed = sum(int(np.prod(a.shape)) * a.dtype.itemsize for a in (*args, *outs))
    vmem, smem, hbm = (pl.BlockSpec(memory_space=m) for m in (pltpu.VMEM, pltpu.SMEM, pltpu.HBM))
    return pl.pallas_call(
        kernel,
        out_shape=outs,
        in_specs=[hbm if i in far else smem if a.ndim == 1 else vmem for i, a in enumerate(args)],
        out_specs=[vmem] * len(outs),
        scratch_shapes=list(scratch),
        compiler_params=pltpu.CompilerParams(vmem_limit_bytes=32 << 20),
        cost_estimate=pl.CostEstimate(flops=flops, bytes_accessed=bytes_accessed, transcendentals=0),
    )(*(pltpu.with_memory_space_constraint(a, pltpu.HBM) if i in far else a for i, a in enumerate(args)))


def shape(dtype, *dims):
    return jax.ShapeDtypeStruct(dims, dtype)


def placement():
    table = np.zeros((NX, 128, NZ // NC, NY, SLICE), np.float32)
    for x in range(NX):
        for lane in range(WIDTH):
            table[x, lane, lane // SLICE, x, lane % SLICE] = 1.0
    return table.reshape(HALF, THIRD)


def columns(wide, width):
    lane = lax.broadcasted_iota(jnp.int32, (128, 128), 1)
    packed = jnp.ones((128, 128), f32)
    for j, group in enumerate(wide):
        for g, column in enumerate(group):
            if column.shape[0] < 128:
                column = jnp.concatenate([column, jnp.ones((128 - column.shape[0], 1), f32)], axis=0)
            packed = jnp.where(lane == 8 * g + j, column, packed)
    return packed.T[:width]


def upright(lines):
    return jnp.concatenate([lines, jnp.zeros((120, 128), f32)], axis=0).T


def prep_kernel(queries_in, positive_in, passages_in, message, queries, positive, passages, wide, tall, sems):
    pairs = ((queries_in, queries), (positive_in, positive), (passages_in, passages))
    copies = [pltpu.make_async_copy(a, b, sems.at[i]) for i, (a, b) in enumerate(pairs)]
    for copy in copies:
        copy.start()
    for copy in copies:
        copy.wait()
    index = positive[...].astype(f32)
    index = jnp.concatenate(
        [index[:, :128], jnp.concatenate([index[:, 128:], jnp.zeros((1, 256 - ROWS), f32)], axis=1)], axis=0
    )
    index = upright(jnp.concatenate([index, jnp.zeros((6, 128), f32)], axis=0))
    index = jnp.concatenate([index[:, 0:1], index[: ROWS - 128, 1:2]], axis=0)
    high = jnp.floor(index * (1.0 / 128.0))
    low = index - 128.0 * high
    wide[...] = jnp.zeros((ROWS, 128), f32)
    wide[:, :WIDTH] = queries[...].astype(f32)
    lane = lax.broadcasted_iota(jnp.int32, (ROWS, 128), 1)
    own = jnp.where(lane == WIDTH, high, jnp.where(lane == WIDTH + 1, low, wide[...])).astype(bf16)
    tall[...] = jnp.zeros((16, COLS), f32)
    tall[:SLICE] = passages[...].astype(f32)
    for y in range(NY):
        message[y, :ROWS] = own
        piece = pltpu.roll(tall[...], (COLS - y * SUB) % COLS, 1)
        for b in range(3):
            message[y, ROWS + 16 * b : ROWS + 16 * b + 16] = piece[:, b * 128 : (b + 1) * 128].astype(bf16)


def split_kernel(came, queries, part, total):
    for y in range(NY):
        for b in range(3):
            piece = came[y, ROWS + 16 * b : ROWS + 16 * b + 16].astype(f32)
            total[y * SLICE : (y + 1) * SLICE, b * 128 : (b + 1) * 128] = piece[:SLICE]
        queries[y * ROWS : (y + 1) * ROWS] = came[y, :ROWS]
    part[...] = total[:, :SUB].astype(bf16)


def tile_kernel(parts, passages, place, row_pairs, col_pairs, placed, targets, query_full, logits, sems):
    copies = [
        pltpu.make_async_copy(parts.at[b], query_full.at[:, pl.ds(b * 128, 128)], sems.at[b])
        for b in range(NC * NX)
    ]
    for copy in copies:
        copy.start()
    for c in range(NC):
        for copy in copies[c * NX : (c + 1) * NX]:
            copy.wait()
        placed[:, c * THIRD : (c + 1) * THIRD] = jnp.dot(
            query_full[:, c * HALF : (c + 1) * HALF], place[...], preferred_element_type=f32
        ).astype(bf16)
    pairs, col_top = [], None
    for start, size in BLOCKS:
        scores = logit_scale * jnp.dot(
            placed[start : start + size], passages[...], preferred_element_type=f32
        )
        logits[start : start + size] = scores
        top = jnp.max(scores, axis=1, keepdims=True)
        pairs.append((top, jnp.sum(jnp.exp(scores - top), axis=1, keepdims=True)))
        peak = jnp.max(scores, axis=0, keepdims=True)
        col_top = peak if col_top is None else jnp.maximum(col_top, peak)
    turned = columns(pairs, 16)
    for i in range(NX * NC):
        row_pairs[i] = turned
    col_sum = jnp.zeros((1, SUB), f32)
    for start, size in BLOCKS:
        col_sum += jnp.sum(jnp.exp(logits[start : start + size] - col_top), axis=0, keepdims=True)
    fill = jnp.ones((1, 384 - SUB), f32)
    both = [jnp.concatenate([v, fill], axis=1) for v in (col_top, col_sum)]
    lines = [v[:, b * 128 : (b + 1) * 128] for v in both for b in range(3)]
    lines = jnp.concatenate(lines + [jnp.ones((2, 128), f32)], axis=0)
    for i in range(NZ):
        col_pairs[i] = lines
    spare = query_full[:, :128].astype(f32)
    target = spare[:, WIDTH : WIDTH + 1] * 128.0 + spare[:, WIDTH + 1 : WIDTH + 2]
    targets[...] = columns([(target[start : start + size],) for start, size in BLOCKS], 8)


def spread_kernel(passages, place, passage_full):
    for c in range(NC):
        turned = jnp.dot(place[...], passages[c * THIRD : (c + 1) * THIRD], preferred_element_type=f32)
        passage_full[c * HALF : (c + 1) * HALF] = turned.astype(bf16)


def passage_kernel(placed, passages, targets, ids, row_pairs, col_pairs, dlogits, terms, tails):
    top, total = row_pairs[:, :8], row_pairs[:, 8:]
    peak = jnp.max(top, axis=0)
    row_lse = upright(peak + jnp.log(jnp.sum(total * jnp.exp(top - peak[None]), axis=0)))
    target = upright(targets[...])
    pairs = col_pairs[...]
    top, total = pairs[:, 0:3], pairs[:, 3:6]
    peak = jnp.max(top, axis=0)
    col_lse = peak + jnp.log(jnp.sum(total * jnp.exp(top - peak[None]), axis=0))
    col_lse = jnp.concatenate([col_lse[b : b + 1] for b in range(3)], axis=1)[:, :SUB]
    dlogits[:, 256:] = jnp.zeros((TALL, 128), bf16)
    for j, (start, size) in enumerate(BLOCKS):
        scores = logit_scale * jnp.dot(placed[start : start + size], passages[...], preferred_element_type=f32)
        slope = jnp.exp(scores - row_lse[:size, j : j + 1]) + jnp.exp(scores - col_lse)
        hit = jnp.where(target[:size, j : j + 1] == ids[...], 2.0, 0.0)
        dlogits[start : start + size, :SUB] = (slope - hit).astype(bf16)
    high = NY * SLICE
    for first in range(0, NZ, 4):
        if first * high % GROUP == 0:
            whole = logit_scale * lax.dot_general(
                placed[:, first * high : first * high + GROUP], dlogits[...], TN, preferred_element_type=f32
            )
        offset = first * high % GROUP
        part = whole[offset : offset + 4 * high]
        for a in range(NY):
            tails[a] = part[:, 256:] if a == 0 else pltpu.roll(part[:, 256:], 32 * a, 1)
        for i in range(4):
            for b in range(2):
                piece = part[i * high : (i + 1) * high, b * 128 : (b + 1) * 128]
                terms[first + i, b * high : (b + 1) * high] = piece.astype(bf16)
            tail = sum(tails[a, i * high + a * SLICE : i * high + (a + 1) * SLICE] for a in range(NY))
            tail = jnp.concatenate([tail, jnp.zeros((16 - SLICE, 128), f32)], axis=0)
            terms[first + i, 2 * high : 2 * high + 16] = tail.astype(bf16)


def theirs_kernel(place, dlogits, passage_full, theirs):
    core = place[0]
    half = passage_full[pl.ds(pl.multiple_of((1 - core) * HALF, HALF), HALF)]
    theirs[...] = logit_scale * lax.dot_general(dlogits[:, :SUB], half, NT, preferred_element_type=f32)


def ours_kernel(place, dlogits, passage_full, theirs, own, *rest):
    outs, total = rest[:-1], rest[-1]
    core, x = place[0], place[1]
    half = passage_full[pl.ds(pl.multiple_of(core * HALF, HALF), HALF)]
    total[...] = theirs[...] + logit_scale * lax.dot_general(
        dlogits[:, :SUB], half, NT, preferred_element_type=f32
    )
    own[...] = total[:, pl.ds(pl.multiple_of(x * 128, 128), 128)]
    for step, out in enumerate(outs, 1):
        lanes = pl.ds(pl.multiple_of(lax.rem(x + step, NX) * 128, 128), 128)
        out[...] = total[:, lanes].astype(bf16)


def fold_kernel(terms, own, *rest):
    came, message, total = rest[:-2], rest[-2], rest[-1]
    high = NY * SLICE
    total[...] = jnp.sum(terms[...].astype(f32), axis=0)
    for y in range(NY):
        rows = slice(y * ROWS, (y + 1) * ROWS)
        message[y, :ROWS] = own[rows] + sum(c[rows].astype(f32) for c in came)
        tail = total[2 * high :]
        tail = tail if y == 0 else pltpu.roll(tail, 128 - 32 * y, 1)
        for b in range(3):
            piece = tail[:SLICE] if b == 2 else total[b * high + y * SLICE : b * high + (y + 1) * SLICE]
            message[y, ROWS + b * 16 : ROWS + b * 16 + SLICE] = piece
            message[y, ROWS + b * 16 + SLICE : ROWS + b * 16 + 16] = jnp.zeros((16 - SLICE, 128), f32)


def final_kernel(came, query_grad, passage_grad):
    query_grad[...] = jnp.sum(came[:, :ROWS], axis=0)[:, :WIDTH]
    lane = lax.broadcasted_iota(jnp.int32, (16, 128), 1)
    total = None
    for y in range(NY):
        blocks = [came[y, ROWS + b * 16 : ROWS + b * 16 + 16] for b in range(3)]
        blocks[2] = jnp.where(lane < SUB - 256, blocks[2], 0.0)
        wide = jnp.concatenate(blocks + [jnp.zeros((16, COLS - 384), f32)], axis=1)
        wide = wide if y == 0 else pltpu.roll(wide, y * SUB, 1)
        total = wide if total is None else total + wide
    passage_grad[...] = total[:SLICE]


def merge(pairs):
    top, total = pairs[:, :8], pairs[:, 8:]
    peak = jnp.max(top, axis=0)
    return jnp.concatenate([peak, jnp.sum(total * jnp.exp(top - peak[None]), axis=0)])


def around(x, axis, n, step):
    return lax.ppermute(x, axis, [(i, (i + step) % n) for i in range(n)])


def body(queries, passages, positive):
    place = jnp.asarray(placement(), bf16)
    where = jnp.stack([lax.axis_index("core"), lax.axis_index("x")]).astype(jnp.int32)

    (message,) = call(
        prep_kernel,
        [shape(bf16, NY, MSG, 128)],
        queries,
        positive[None],
        passages.T,
        far=(0, 1, 2),
        scratch=[
            pltpu.VMEM((ROWS, WIDTH), bf16),
            pltpu.VMEM((1, ROWS), jnp.int32),
            pltpu.VMEM((SLICE, COLS), bf16),
            pltpu.VMEM((ROWS, 128), f32),
            pltpu.VMEM((16, COLS), f32),
            pltpu.SemaphoreType.DMA((3,)),
        ],
    )
    message = lax.all_to_all(message, "y", 0, 0, tiled=True)
    parts, passage_part = call(
        split_kernel,
        [shape(bf16, TALL, 128), shape(bf16, NY * SLICE, SUB)],
        message,
        scratch=[pltpu.VMEM((NY * SLICE, 384), f32)],
    )
    parts = lax.all_gather(parts, ("core", "x"))
    passage_part = lax.all_gather(passage_part, "z", axis=0, tiled=True)

    row_pairs, col_pairs, placed, targets = call(
        tile_kernel,
        [
            shape(f32, NX * NC, 16, 128),
            shape(f32, NZ, 8, 128),
            shape(bf16, TALL, NC * THIRD),
            shape(f32, 8, 128),
        ],
        parts,
        passage_part,
        place,
        far=(0,),
        scratch=[
            pltpu.VMEM((TALL, NC * HALF), bf16),
            pltpu.VMEM((TALL, SUB), f32),
            pltpu.SemaphoreType.DMA((NC * NX,)),
        ],
        flops=2 * TALL * SUB * NC * HALF,
    )
    passage_part, targets = lax.optimization_barrier((passage_part, targets))
    (passage_full,) = call(
        spread_kernel,
        [shape(bf16, NC * HALF, SUB)],
        passage_part,
        place,
        flops=2 * NC * HALF * THIRD * SUB,
    )
    col_pairs, passage_full = lax.optimization_barrier((col_pairs, passage_full))
    row_pairs = lax.all_to_all(row_pairs, ("x", "core"), 0, 0, tiled=True)
    col_pairs = lax.all_to_all(col_pairs, "z", 0, 0, tiled=True)
    row_pairs = lax.all_gather(merge(row_pairs), "y")

    block = (lax.axis_index("x") * NC + lax.axis_index("core")) * NY + lax.axis_index("y")
    ids = (block * SUB + jnp.arange(SUB, dtype=jnp.int32)).astype(f32)[None]
    dlogits, terms = call(
        passage_kernel,
        [shape(bf16, TALL, 384), shape(bf16, NZ, 112, 128)],
        placed,
        passage_part,
        targets,
        ids,
        row_pairs,
        col_pairs,
        scratch=[pltpu.VMEM((NY, 4 * NY * SLICE, 128), f32)],
        flops=2 * TALL * SUB * NC * THIRD,
    )
    terms = lax.all_to_all(terms, "z", 0, 0, tiled=True)

    (theirs,) = call(
        theirs_kernel, [shape(f32, TALL, HALF)], where, dlogits, passage_full, flops=2 * TALL * SUB * HALF
    )
    theirs = around(theirs, "core", NC, 1)
    own, *others = call(
        ours_kernel,
        [shape(f32, TALL, 128)] + [shape(bf16, TALL, 128)] * (NX - 1),
        where,
        dlogits,
        passage_full,
        theirs,
        scratch=[pltpu.VMEM((TALL, HALF), f32)],
        flops=2 * TALL * SUB * HALF,
    )
    came = [around(other, "x", NX, step) for step, other in enumerate(others, 1)]

    (message,) = call(fold_kernel, [shape(f32, NY, MSG, 128)], terms, own, *came, scratch=[pltpu.VMEM((112, 128), f32)])
    message = lax.all_to_all(message, "y", 0, 0, tiled=True)
    query_grad, passage_grad = call(final_kernel, [shape(f32, ROWS, WIDTH), shape(f32, SLICE, COLS)], message)
    return (query_grad, passage_grad.T)


def solution(mesh):
    chips = Mesh(mesh.devices.reshape(NY, NZ, NX, NC), ("y", "z", "x", "core"))
    yz, xc = ("y", "z"), ("x", "core")
    return jax.shard_map(
        body,
        mesh=chips,
        in_specs=(P(yz, xc), P(xc, yz), P(yz)),
        out_specs=(P(yz, xc), P(xc, yz)),
        check_vma=False,
    )
```

```python
import jax
import jax.numpy as jnp
import numpy as np
from jax import lax
from jax.experimental import pallas as pl
from jax.experimental.pallas import tpu as pltpu
from jax.sharding import Mesh, PartitionSpec as P

logit_scale = 20.0
f32 = jnp.float32
bf16 = jnp.bfloat16
NY, NZ, NX, NC = 4, 16, 4, 2
ROWS, WIDTH = 144, 96
COLS, SLICE = 1152, 12
TALL, SUB = NY * ROWS, COLS // NY
HALF = NX * 128
THIRD = NZ * NY * SLICE // NC
BLOCKS = [(0, 128), (128, 128), (256, 128), (384, 128), (512, 64)]
MSG = ROWS + 48
QUARTER = ROWS // 4
GROUP = 384
NT = (((1,), (1,)), ((), ()))
TN = (((0,), (0,)), ((), ()))


def call(kernel, outs, *args, far=(), scratch=(), flops=0):
    bytes_accessed = sum(int(np.prod(a.shape)) * a.dtype.itemsize for a in (*args, *outs))
    vmem, smem, hbm = (pl.BlockSpec(memory_space=m) for m in (pltpu.VMEM, pltpu.SMEM, pltpu.HBM))
    return pl.pallas_call(
        kernel,
        out_shape=outs,
        in_specs=[hbm if i in far else smem if a.ndim == 1 else vmem for i, a in enumerate(args)],
        out_specs=[vmem] * len(outs),
        scratch_shapes=list(scratch),
        compiler_params=pltpu.CompilerParams(vmem_limit_bytes=32 << 20),
        cost_estimate=pl.CostEstimate(flops=flops, bytes_accessed=bytes_accessed, transcendentals=0),
    )(*(pltpu.with_memory_space_constraint(a, pltpu.HBM) if i in far else a for i, a in enumerate(args)))


def shape(dtype, *dims):
    return jax.ShapeDtypeStruct(dims, dtype)


def placement():
    table = np.zeros((NX, 128, NZ // NC, NY, SLICE), np.float32)
    for x in range(NX):
        for lane in range(WIDTH):
            table[x, lane, lane // SLICE, x, lane % SLICE] = 1.0
    return table.reshape(HALF, THIRD)


def columns(wide, width):
    lane = lax.broadcasted_iota(jnp.int32, (128, 128), 1)
    packed = jnp.ones((128, 128), f32)
    for j, group in enumerate(wide):
        for g, column in enumerate(group):
            if column.shape[0] < 128:
                column = jnp.concatenate([column, jnp.ones((128 - column.shape[0], 1), f32)], axis=0)
            packed = jnp.where(lane == 8 * g + j, column, packed)
    return packed.T[:width]


def upright(lines):
    return jnp.concatenate([lines, jnp.zeros((120, 128), f32)], axis=0).T


def prep_kernel(queries_in, positive_in, passages_in, message, queries, positive, passages, wide, tall, sems):
    pairs = ((queries_in, queries), (positive_in, positive), (passages_in, passages))
    copies = [pltpu.make_async_copy(a, b, sems.at[i]) for i, (a, b) in enumerate(pairs)]
    for copy in copies:
        copy.start()
    for copy in copies:
        copy.wait()
    index = positive[...].astype(f32)
    index = jnp.concatenate(
        [index[:, :128], jnp.concatenate([index[:, 128:], jnp.zeros((1, 256 - ROWS), f32)], axis=1)], axis=0
    )
    index = upright(jnp.concatenate([index, jnp.zeros((6, 128), f32)], axis=0))
    index = jnp.concatenate([index[:, 0:1], index[: ROWS - 128, 1:2]], axis=0)
    high = jnp.floor(index * (1.0 / 128.0))
    low = index - 128.0 * high
    wide[...] = jnp.zeros((ROWS, 128), f32)
    wide[:, :WIDTH] = queries[...].astype(f32)
    lane = lax.broadcasted_iota(jnp.int32, (ROWS, 128), 1)
    own = jnp.where(lane == WIDTH, high, jnp.where(lane == WIDTH + 1, low, wide[...])).astype(bf16)
    tall[...] = jnp.zeros((16, COLS), f32)
    tall[:SLICE] = passages[...].astype(f32)
    for y in range(NY):
        message[y, :ROWS] = own
        piece = pltpu.roll(tall[...], (COLS - y * SUB) % COLS, 1)
        for b in range(3):
            message[y, ROWS + 16 * b : ROWS + 16 * b + 16] = piece[:, b * 128 : (b + 1) * 128].astype(bf16)


def split_kernel(came, queries, part, total):
    for y in range(NY):
        for b in range(3):
            piece = came[y, ROWS + 16 * b : ROWS + 16 * b + 16].astype(f32)
            total[y * SLICE : (y + 1) * SLICE, b * 128 : (b + 1) * 128] = piece[:SLICE]
        for i in range(NX * NC):
            queries[i, y * ROWS : (y + 1) * ROWS] = came[y, :ROWS]
    part[...] = total[:, :SUB].astype(bf16)


def tile_kernel(parts, passages, place, row_pairs, col_pairs, placed, targets, query_half, logits):
    for c in range(NC):
        for x in range(NX):
            query_half[:, x * 128 : (x + 1) * 128] = parts[c * NX + x]
        placed[:, c * THIRD : (c + 1) * THIRD] = jnp.dot(
            query_half[...], place[...], preferred_element_type=f32
        ).astype(bf16)
    pairs, col_top = [], None
    for start, size in BLOCKS:
        scores = logit_scale * jnp.dot(
            placed[start : start + size], passages[...], preferred_element_type=f32
        )
        logits[start : start + size] = scores
        top = jnp.max(scores, axis=1, keepdims=True)
        pairs.append((top, jnp.sum(jnp.exp(scores - top), axis=1, keepdims=True)))
        peak = jnp.max(scores, axis=0, keepdims=True)
        col_top = peak if col_top is None else jnp.maximum(col_top, peak)
    turned = columns(pairs, 16)
    for i in range(NX * NC):
        row_pairs[i] = turned
    col_sum = jnp.zeros((1, SUB), f32)
    for start, size in BLOCKS:
        col_sum += jnp.sum(jnp.exp(logits[start : start + size] - col_top), axis=0, keepdims=True)
    fill = jnp.ones((1, 384 - SUB), f32)
    both = [jnp.concatenate([v, fill], axis=1) for v in (col_top, col_sum)]
    lines = [v[:, b * 128 : (b + 1) * 128] for v in both for b in range(3)]
    lines = jnp.concatenate(lines + [jnp.ones((2, 128), f32)], axis=0)
    for i in range(NZ):
        col_pairs[i] = lines
    spare = parts[0].astype(f32)
    target = spare[:, WIDTH : WIDTH + 1] * 128.0 + spare[:, WIDTH + 1 : WIDTH + 2]
    targets[...] = columns([(target[start : start + size],) for start, size in BLOCKS], 8)


def spread_kernel(where, passages, place, own_half, other_half):
    for c, half in ((where[0], own_half), (1 - where[0], other_half)):
        rows = pl.ds(pl.multiple_of(c * THIRD, THIRD), THIRD)
        half[...] = jnp.dot(place[...], passages[rows], preferred_element_type=f32).astype(bf16)


def passage_kernel(placed, passages, targets, ids, row_pairs, col_pairs, dlogits, terms, tails):
    top, total = row_pairs[:, :8], row_pairs[:, 8:]
    peak = jnp.max(top, axis=0)
    row_lse = upright(peak + jnp.log(jnp.sum(total * jnp.exp(top - peak[None]), axis=0)))
    target = upright(targets[...])
    pairs = col_pairs[...]
    top, total = pairs[:, 0:3], pairs[:, 3:6]
    peak = jnp.max(top, axis=0)
    col_lse = peak + jnp.log(jnp.sum(total * jnp.exp(top - peak[None]), axis=0))
    col_lse = jnp.concatenate([col_lse[b : b + 1] for b in range(3)], axis=1)[:, :SUB]
    dlogits[:, 256:] = jnp.zeros((TALL, 128), bf16)
    for j, (start, size) in enumerate(BLOCKS):
        scores = logit_scale * jnp.dot(placed[start : start + size], passages[...], preferred_element_type=f32)
        slope = jnp.exp(scores - row_lse[:size, j : j + 1]) + jnp.exp(scores - col_lse)
        hit = jnp.where(target[:size, j : j + 1] == ids[...], 2.0, 0.0)
        dlogits[start : start + size, :SUB] = (slope - hit).astype(bf16)
    high = NY * SLICE
    for first in range(0, NZ, 4):
        if first * high % GROUP == 0:
            whole = logit_scale * lax.dot_general(
                placed[:, first * high : first * high + GROUP], dlogits[...], TN, preferred_element_type=f32
            )
        offset = first * high % GROUP
        part = whole[offset : offset + 4 * high]
        for a in range(NY):
            tails[a] = part[:, 256:] if a == 0 else pltpu.roll(part[:, 256:], 32 * a, 1)
        for i in range(4):
            for b in range(2):
                piece = part[i * high : (i + 1) * high, b * 128 : (b + 1) * 128]
                terms[first + i, b * high : (b + 1) * high] = piece.astype(bf16)
            tail = sum(tails[a, i * high + a * SLICE : i * high + (a + 1) * SLICE] for a in range(NY))
            tail = jnp.concatenate([tail, jnp.zeros((16 - SLICE, 128), f32)], axis=0)
            terms[first + i, 2 * high : 2 * high + 16] = tail.astype(bf16)


def squeeze(block):
    lane = lax.broadcasted_iota(jnp.int32, (ROWS, 128), 1)
    tail = block[3 * ROWS :]
    parts = []
    for j in range(3):
        moved = pltpu.roll(tail, WIDTH - 32 * j, 1)
        parts.append(jnp.where(lane < WIDTH, block[j * ROWS : (j + 1) * ROWS], moved))
    return jnp.concatenate(parts, axis=0)


def query_kernel(where, dlogits, other_dlogits, own_half, other_half, own, *rest):
    outs, total = rest[:-1], rest[-1]
    total[...] = logit_scale * (
        lax.dot_general(dlogits[:, :SUB], own_half[...], NT, preferred_element_type=f32)
        + lax.dot_general(other_dlogits[:, :SUB], other_half[...], NT, preferred_element_type=f32)
    )
    own[...] = squeeze(total[:, pl.ds(pl.multiple_of(where[1] * 128, 128), 128)])
    for step, out in enumerate(outs, 1):
        lanes = pl.ds(pl.multiple_of(lax.rem(where[1] + step, NX) * 128, 128), 128)
        out[...] = squeeze(total[:, lanes]).astype(bf16)


def fold_kernel(terms, own, *rest):
    came, message, total, block = rest[:-3], rest[-3], rest[-2], rest[-1]
    high = NY * SLICE
    total[...] = jnp.sum(terms[...].astype(f32), axis=0)
    lane = lax.broadcasted_iota(jnp.int32, (ROWS, 128), 1)
    short = lax.broadcasted_iota(jnp.int32, (QUARTER, 128), 1)
    last = jnp.zeros((ROWS, 128), f32)
    for y in range(NY):
        if y < 3:
            rows = slice(y * ROWS, (y + 1) * ROWS)
            value = own[rows] + sum(c[rows].astype(f32) for c in came)
            moved = pltpu.roll(value, (128 + 32 * y - WIDTH) % 128, 1)
            last = jnp.where((lane >= 32 * y) & (lane < 32 * y + 32), moved, last)
        else:
            value = last
        block[...] = value
        extra = block[3 * QUARTER :]
        for j in range(3):
            moved = pltpu.roll(extra, WIDTH - 32 * j, 1)
            piece = block[j * QUARTER : (j + 1) * QUARTER]
            message[y, j * QUARTER : (j + 1) * QUARTER] = jnp.where(short < WIDTH, piece, moved)
        tail = total[2 * high :]
        tail = tail if y == 0 else pltpu.roll(tail, 128 - 32 * y, 1)
        for b in range(3):
            piece = tail[:SLICE] if b == 2 else total[b * high + y * SLICE : b * high + (y + 1) * SLICE]
            message[y, 3 * QUARTER + b * SLICE : 3 * QUARTER + (b + 1) * SLICE] = piece


def final_kernel(came, query_grad, passage_grad, total):
    total[...] = jnp.sum(came[:, : 3 * QUARTER], axis=0)
    short = lax.broadcasted_iota(jnp.int32, (QUARTER, 128), 1)
    last = jnp.zeros((QUARTER, 128), f32)
    for j in range(3):
        rows = slice(j * QUARTER, (j + 1) * QUARTER)
        query_grad[rows] = total[rows, :WIDTH]
        moved = pltpu.roll(total[rows], (128 + 32 * j - WIDTH) % 128, 1)
        last = jnp.where((short >= 32 * j) & (short < 32 * j + 32), moved, last)
    query_grad[3 * QUARTER :] = last[:, :WIDTH]
    lane = lax.broadcasted_iota(jnp.int32, (SLICE, 128), 1)
    wide = None
    for y in range(NY):
        first = 3 * QUARTER
        blocks = [came[y, first + b * SLICE : first + (b + 1) * SLICE] for b in range(3)]
        blocks[2] = jnp.where(lane < SUB - 256, blocks[2], 0.0)
        row = jnp.concatenate(blocks + [jnp.zeros((SLICE, COLS - 384), f32)], axis=1)
        row = jnp.concatenate([row, jnp.zeros((16 - SLICE, COLS), f32)], axis=0)
        row = row if y == 0 else pltpu.roll(row, y * SUB, 1)
        wide = row if wide is None else wide + row
    passage_grad[...] = wide[:SLICE]


def merge(pairs):
    top, total = pairs[:, :8], pairs[:, 8:]
    peak = jnp.max(top, axis=0)
    return jnp.concatenate([peak, jnp.sum(total * jnp.exp(top - peak[None]), axis=0)])


def around(x, axis, n, step):
    return lax.ppermute(x, axis, [(i, (i + step) % n) for i in range(n)])


def body(queries, passages, positive):
    place = jnp.asarray(placement(), bf16)
    where = jnp.stack([lax.axis_index("core"), lax.axis_index("x")]).astype(jnp.int32)

    (message,) = call(
        prep_kernel,
        [shape(bf16, NY, MSG, 128)],
        queries,
        positive[None],
        passages.T,
        far=(0, 1, 2),
        scratch=[
            pltpu.VMEM((ROWS, WIDTH), bf16),
            pltpu.VMEM((1, ROWS), jnp.int32),
            pltpu.VMEM((SLICE, COLS), bf16),
            pltpu.VMEM((ROWS, 128), f32),
            pltpu.VMEM((16, COLS), f32),
            pltpu.SemaphoreType.DMA((3,)),
        ],
    )
    message = lax.all_to_all(message, "y", 0, 0, tiled=True)
    parts, passage_part = call(
        split_kernel,
        [shape(bf16, NX * NC, TALL, 128), shape(bf16, NY * SLICE, SUB)],
        message,
        scratch=[pltpu.VMEM((NY * SLICE, 384), f32)],
    )
    parts = lax.all_to_all(parts, ("core", "x"), 0, 0, tiled=True)
    passage_part = lax.all_gather(passage_part, "z", axis=0, tiled=True)

    row_pairs, col_pairs, placed, targets = call(
        tile_kernel,
        [
            shape(f32, NX * NC, 16, 128),
            shape(f32, NZ, 8, 128),
            shape(bf16, TALL, NC * THIRD),
            shape(f32, 8, 128),
        ],
        parts,
        passage_part,
        place,
        scratch=[pltpu.VMEM((TALL, HALF), bf16), pltpu.VMEM((TALL, SUB), f32)],
        flops=2 * TALL * SUB * NC * HALF,
    )
    passage_part, targets = lax.optimization_barrier((passage_part, targets))
    own_half, other_half = call(
        spread_kernel,
        [shape(bf16, HALF, SUB)] * 2,
        where,
        passage_part,
        place,
        flops=2 * NC * HALF * THIRD * SUB,
    )
    other_half = around(other_half, "core", NC, 1)
    col_pairs, own_half = lax.optimization_barrier((col_pairs, own_half))
    targets, other_half = lax.optimization_barrier((targets, other_half))
    row_pairs = lax.all_to_all(row_pairs, ("x", "core"), 0, 0, tiled=True)
    col_pairs = lax.all_to_all(col_pairs, "z", 0, 0, tiled=True)
    row_pairs = lax.all_gather(merge(row_pairs), "y")

    block = (lax.axis_index("x") * NC + lax.axis_index("core")) * NY + lax.axis_index("y")
    ids = (block * SUB + jnp.arange(SUB, dtype=jnp.int32)).astype(f32)[None]
    dlogits, terms = call(
        passage_kernel,
        [shape(bf16, TALL, 384), shape(bf16, NZ, 112, 128)],
        placed,
        passage_part,
        targets,
        ids,
        row_pairs,
        col_pairs,
        scratch=[pltpu.VMEM((NY, 4 * NY * SLICE, 128), f32)],
        flops=2 * TALL * SUB * NC * THIRD,
    )
    terms = lax.all_to_all(terms, "z", 0, 0, tiled=True)

    own, *others = call(
        query_kernel,
        [shape(f32, 3 * ROWS, 128)] + [shape(bf16, 3 * ROWS, 128)] * (NX - 1),
        where,
        dlogits,
        around(dlogits, "core", NC, 1),
        own_half,
        other_half,
        scratch=[pltpu.VMEM((TALL, HALF), f32)],
        flops=4 * TALL * SUB * HALF,
    )
    came = [around(other, "x", NX, step) for step, other in enumerate(others, 1)]

    (message,) = call(
        fold_kernel,
        [shape(f32, NY, ROWS, 128)],
        terms,
        own,
        *came,
        scratch=[pltpu.VMEM((112, 128), f32), pltpu.VMEM((ROWS, 128), f32)],
    )
    message = lax.all_to_all(message, "y", 0, 0, tiled=True)
    query_grad, passage_grad = call(
        final_kernel,
        [shape(f32, ROWS, WIDTH), shape(f32, SLICE, COLS)],
        message,
        scratch=[pltpu.VMEM((3 * QUARTER, 128), f32)],
    )
    return (query_grad, passage_grad.T)


def solution(mesh):
    chips = Mesh(mesh.devices.reshape(NY, NZ, NX, NC), ("y", "z", "x", "core"))
    yz, xc = ("y", "z"), ("x", "core")
    return jax.shard_map(
        body,
        mesh=chips,
        in_specs=(P(yz, xc), P(xc, yz), P(yz)),
        out_specs=(P(yz, xc), P(xc, yz)),
        check_vma=False,
    )
```

```python
import jax
import jax.numpy as jnp
import numpy as np
from jax import lax
from jax.experimental import pallas as pl
from jax.experimental.pallas import tpu as pltpu
from jax.sharding import Mesh, PartitionSpec as P

logit_scale = 20.0
f32 = jnp.float32
bf16 = jnp.bfloat16
NY, NZ, NX, NC = 4, 16, 4, 2
ROWS, WIDTH = 144, 96
COLS, SLICE = 1152, 12
TALL, SUB = NY * ROWS, COLS // NY
HALF = NX * 128
THIRD = NZ * NY * SLICE // NC
BLOCKS = [(0, 128), (128, 128), (256, 128), (384, 128), (512, 64)]
MSG = ROWS + 48
QUARTER = ROWS // 4
GROUP = 384
NT = (((1,), (1,)), ((), ()))
TN = (((0,), (0,)), ((), ()))


def call(kernel, outs, *args, far=(), far_outs=(), scratch=(), flops=0):
    bytes_accessed = sum(int(np.prod(a.shape)) * a.dtype.itemsize for a in (*args, *outs))
    vmem, smem, hbm = (pl.BlockSpec(memory_space=m) for m in (pltpu.VMEM, pltpu.SMEM, pltpu.HBM))
    return pl.pallas_call(
        kernel,
        out_shape=[pltpu.HBM(o.shape, o.dtype) if i in far_outs else o for i, o in enumerate(outs)],
        in_specs=[hbm if i in far else smem if a.ndim == 1 else vmem for i, a in enumerate(args)],
        out_specs=[hbm if i in far_outs else vmem for i in range(len(outs))],
        scratch_shapes=list(scratch),
        compiler_params=pltpu.CompilerParams(vmem_limit_bytes=32 << 20),
        cost_estimate=pl.CostEstimate(flops=flops, bytes_accessed=bytes_accessed, transcendentals=0),
    )(*(pltpu.with_memory_space_constraint(a, pltpu.HBM) if i in far else a for i, a in enumerate(args)))


def shape(dtype, *dims):
    return jax.ShapeDtypeStruct(dims, dtype)


def placement():
    table = np.zeros((NX, 128, NZ // NC, NY, SLICE), np.float32)
    for x in range(NX):
        for lane in range(WIDTH):
            table[x, lane, lane // SLICE, x, lane % SLICE] = 1.0
    return table.reshape(HALF, THIRD)


def columns(wide, width):
    lane = lax.broadcasted_iota(jnp.int32, (128, 128), 1)
    packed = jnp.ones((128, 128), f32)
    for j, group in enumerate(wide):
        for g, column in enumerate(group):
            if column.shape[0] < 128:
                column = jnp.concatenate([column, jnp.ones((128 - column.shape[0], 1), f32)], axis=0)
            packed = jnp.where(lane == 8 * g + j, column, packed)
    return packed.T[:width]


def upright(lines):
    return jnp.concatenate([lines, jnp.zeros((120, 128), f32)], axis=0).T


def prep_kernel(queries_in, positive_in, passages_in, message, queries, positive, passages, wide, tall, sems):
    pairs = ((queries_in, queries), (positive_in, positive), (passages_in, passages))
    copies = [pltpu.make_async_copy(a, b, sems.at[i]) for i, (a, b) in enumerate(pairs)]
    for copy in copies:
        copy.start()
    for copy in copies:
        copy.wait()
    index = positive[...].astype(f32)
    index = jnp.concatenate(
        [index[:, :128], jnp.concatenate([index[:, 128:], jnp.zeros((1, 256 - ROWS), f32)], axis=1)], axis=0
    )
    index = upright(jnp.concatenate([index, jnp.zeros((6, 128), f32)], axis=0))
    index = jnp.concatenate([index[:, 0:1], index[: ROWS - 128, 1:2]], axis=0)
    high = jnp.floor(index * (1.0 / 128.0))
    low = index - 128.0 * high
    wide[...] = jnp.zeros((ROWS, 128), f32)
    wide[:, :WIDTH] = queries[...].astype(f32)
    lane = lax.broadcasted_iota(jnp.int32, (ROWS, 128), 1)
    own = jnp.where(lane == WIDTH, high, jnp.where(lane == WIDTH + 1, low, wide[...])).astype(bf16)
    tall[...] = jnp.zeros((16, COLS), f32)
    tall[:SLICE] = passages[...].astype(f32)
    for y in range(NY):
        message[y, :ROWS] = own
        piece = pltpu.roll(tall[...], (COLS - y * SUB) % COLS, 1)
        for b in range(3):
            message[y, ROWS + 16 * b : ROWS + 16 * b + 16] = piece[:, b * 128 : (b + 1) * 128].astype(bf16)


def split_kernel(came, queries, part, total, sems):
    copies = [
        pltpu.make_async_copy(
            came.at[y, pl.ds(0, ROWS)], queries.at[i, pl.ds(y * ROWS, ROWS)], sems.at[y * NX * NC + i]
        )
        for y in range(NY)
        for i in range(NX * NC)
    ]
    for copy in copies:
        copy.start()
    for y in range(NY):
        for b in range(3):
            piece = came[y, ROWS + 16 * b : ROWS + 16 * b + 16].astype(f32)
            total[y * SLICE : (y + 1) * SLICE, b * 128 : (b + 1) * 128] = piece[:SLICE]
    high = NY * SLICE
    for b in range(2):
        part[b * high : (b + 1) * high] = total[:, b * 128 : (b + 1) * 128].astype(bf16)
    lane = lax.broadcasted_iota(jnp.int32, (SLICE, 128), 1)
    tail = jnp.zeros((SLICE, 128), f32)
    for y in range(NY):
        piece = jnp.where(lane < SUB - 256, total[y * SLICE : (y + 1) * SLICE, 256:], 0.0)
        tail += piece if y == 0 else pltpu.roll(piece, 32 * y, 1)
    tail = jnp.concatenate([tail, jnp.zeros((16 - SLICE, 128), f32)], axis=0)
    part[2 * high :] = tail.astype(bf16)
    for copy in copies:
        copy.wait()


def unpack(came, passages, tails):
    high = NY * SLICE
    for z in range(NZ):
        for b in range(2):
            passages[z * high : (z + 1) * high, b * 128 : (b + 1) * 128] = came[z, b * high : (b + 1) * high]
    packed = came[:, 2 * high :].astype(f32).reshape(NZ * 16, 128)
    for y in range(NY):
        moved = packed if y == 0 else pltpu.roll(packed, 128 - 32 * y, 1)
        for z in range(NZ):
            tails[z * high + y * SLICE : z * high + (y + 1) * SLICE] = moved[z * 16 : z * 16 + SLICE]
    passages[:, 256:] = tails[:, : SUB - 256].astype(bf16)


def tile_kernel(
    parts, came, place, passages, row_pairs, col_pairs, placed, targets, query_half, logits, tails, rows, cols, sems
):
    unpack(came, passages, tails)
    for c in range(NC):
        for x in range(NX):
            query_half[:, x * 128 : (x + 1) * 128] = parts[c * NX + x]
        placed[:, c * THIRD : (c + 1) * THIRD] = jnp.dot(
            query_half[...], place[...], preferred_element_type=f32
        ).astype(bf16)
    pairs, col_top = [], None
    for start, size in BLOCKS:
        scores = logit_scale * jnp.dot(
            placed[start : start + size], passages[...], preferred_element_type=f32
        )
        logits[start : start + size] = scores
        top = jnp.max(scores, axis=1, keepdims=True)
        pairs.append((top, jnp.sum(jnp.exp(scores - top), axis=1, keepdims=True)))
        peak = jnp.max(scores, axis=0, keepdims=True)
        col_top = peak if col_top is None else jnp.maximum(col_top, peak)
    rows[...] = columns(pairs, 16)
    copies = [pltpu.make_async_copy(rows, row_pairs.at[i], sems.at[i]) for i in range(NX * NC)]
    for copy in copies:
        copy.start()
    col_sum = jnp.zeros((1, SUB), f32)
    for start, size in BLOCKS:
        col_sum += jnp.sum(jnp.exp(logits[start : start + size] - col_top), axis=0, keepdims=True)
    fill = jnp.ones((1, 384 - SUB), f32)
    both = [jnp.concatenate([v, fill], axis=1) for v in (col_top, col_sum)]
    lines = [v[:, b * 128 : (b + 1) * 128] for v in both for b in range(3)]
    cols[...] = jnp.concatenate(lines + [jnp.ones((2, 128), f32)], axis=0)
    for i in range(NZ):
        copies.append(pltpu.make_async_copy(cols, col_pairs.at[i], sems.at[NX * NC + i]))
        copies[-1].start()
    spare = parts[0].astype(f32)
    target = spare[:, WIDTH : WIDTH + 1] * 128.0 + spare[:, WIDTH + 1 : WIDTH + 2]
    targets[...] = columns([(target[start : start + size],) for start, size in BLOCKS], 8)
    for copy in copies:
        copy.wait()


def spread_kernel(where, passages, place, own_half, other_half):
    for c, half in ((where[0], own_half), (1 - where[0], other_half)):
        rows = pl.ds(pl.multiple_of(c * THIRD, THIRD), THIRD)
        half[...] = jnp.dot(place[...], passages[rows], preferred_element_type=f32).astype(bf16)


def passage_kernel(placed, passages, targets, ids, row_pairs, col_pairs, dlogits, out, tails, terms, sems):
    top, total = row_pairs[:, :8], row_pairs[:, 8:]
    peak = jnp.max(top, axis=0)
    row_lse = upright(peak + jnp.log(jnp.sum(total * jnp.exp(top - peak[None]), axis=0)))
    target = upright(targets[...])
    pairs = col_pairs[...]
    top, total = pairs[:, 0:3], pairs[:, 3:6]
    peak = jnp.max(top, axis=0)
    col_lse = peak + jnp.log(jnp.sum(total * jnp.exp(top - peak[None]), axis=0))
    col_lse = jnp.concatenate([col_lse[b : b + 1] for b in range(3)], axis=1)[:, :SUB]
    dlogits[:, 256:] = jnp.zeros((TALL, 128), bf16)
    for j, (start, size) in enumerate(BLOCKS):
        scores = logit_scale * jnp.dot(placed[start : start + size], passages[...], preferred_element_type=f32)
        slope = jnp.exp(scores - row_lse[:size, j : j + 1]) + jnp.exp(scores - col_lse)
        hit = jnp.where(target[:size, j : j + 1] == ids[...], 2.0, 0.0)
        dlogits[start : start + size, :SUB] = (slope - hit).astype(bf16)
    high = NY * SLICE
    copies = []
    for first in range(0, NZ, 4):
        if first * high % GROUP == 0:
            whole = logit_scale * lax.dot_general(
                placed[:, first * high : first * high + GROUP], dlogits[...], TN, preferred_element_type=f32
            )
        offset = first * high % GROUP
        part = whole[offset : offset + 4 * high]
        for a in range(NY):
            tails[a] = part[:, 256:] if a == 0 else pltpu.roll(part[:, 256:], 32 * a, 1)
        for i in range(4):
            for b in range(2):
                piece = part[i * high : (i + 1) * high, b * 128 : (b + 1) * 128]
                terms[first + i, b * high : (b + 1) * high] = piece.astype(bf16)
            tail = sum(tails[a, i * high + a * SLICE : i * high + (a + 1) * SLICE] for a in range(NY))
            tail = jnp.concatenate([tail, jnp.zeros((16 - SLICE, 128), f32)], axis=0)
            terms[first + i, 2 * high : 2 * high + 16] = tail.astype(bf16)
        group = pl.ds(first, 4)
        copies.append(pltpu.make_async_copy(terms.at[group], out.at[group], sems.at[first // 4]))
        copies[-1].start()
    for copy in copies:
        copy.wait()


def squeeze(block):
    lane = lax.broadcasted_iota(jnp.int32, (ROWS, 128), 1)
    tail = block[3 * ROWS :]
    parts = []
    for j in range(3):
        moved = pltpu.roll(tail, WIDTH - 32 * j, 1)
        parts.append(jnp.where(lane < WIDTH, block[j * ROWS : (j + 1) * ROWS], moved))
    return jnp.concatenate(parts, axis=0)


def query_kernel(where, dlogits, other_dlogits, own_half, other_half, own, *rest):
    outs, total = rest[:-1], rest[-1]
    total[...] = logit_scale * (
        lax.dot_general(dlogits[:, :SUB], own_half[...], NT, preferred_element_type=f32)
        + lax.dot_general(other_dlogits[:, :SUB], other_half[...], NT, preferred_element_type=f32)
    )
    own[...] = squeeze(total[:, pl.ds(pl.multiple_of(where[1] * 128, 128), 128)])
    for step, out in enumerate(outs, 1):
        lanes = pl.ds(pl.multiple_of(lax.rem(where[1] + step, NX) * 128, 128), 128)
        out[...] = squeeze(total[:, lanes]).astype(bf16)


def fold_kernel(terms, own, *rest):
    came, message, total, block = rest[:-3], rest[-3], rest[-2], rest[-1]
    high = NY * SLICE
    total[...] = jnp.sum(terms[...].astype(f32), axis=0)
    lane = lax.broadcasted_iota(jnp.int32, (ROWS, 128), 1)
    short = lax.broadcasted_iota(jnp.int32, (QUARTER, 128), 1)
    last = jnp.zeros((ROWS, 128), f32)
    for y in range(NY):
        if y < 3:
            rows = slice(y * ROWS, (y + 1) * ROWS)
            value = own[rows] + sum(c[rows].astype(f32) for c in came)
            moved = pltpu.roll(value, (128 + 32 * y - WIDTH) % 128, 1)
            last = jnp.where((lane >= 32 * y) & (lane < 32 * y + 32), moved, last)
        else:
            value = last
        block[...] = value
        extra = block[3 * QUARTER :]
        for j in range(3):
            moved = pltpu.roll(extra, WIDTH - 32 * j, 1)
            piece = block[j * QUARTER : (j + 1) * QUARTER]
            message[y, j * QUARTER : (j + 1) * QUARTER] = jnp.where(short < WIDTH, piece, moved)
        tail = total[2 * high :]
        tail = tail if y == 0 else pltpu.roll(tail, 128 - 32 * y, 1)
        for b in range(3):
            piece = tail[:SLICE] if b == 2 else total[b * high + y * SLICE : b * high + (y + 1) * SLICE]
            message[y, 3 * QUARTER + b * SLICE : 3 * QUARTER + (b + 1) * SLICE] = piece


def final_kernel(came, query_grad, passage_grad, total):
    total[...] = jnp.sum(came[:, : 3 * QUARTER], axis=0)
    short = lax.broadcasted_iota(jnp.int32, (QUARTER, 128), 1)
    last = jnp.zeros((QUARTER, 128), f32)
    for j in range(3):
        rows = slice(j * QUARTER, (j + 1) * QUARTER)
        query_grad[rows] = total[rows, :WIDTH]
        moved = pltpu.roll(total[rows], (128 + 32 * j - WIDTH) % 128, 1)
        last = jnp.where((short >= 32 * j) & (short < 32 * j + 32), moved, last)
    query_grad[3 * QUARTER :] = last[:, :WIDTH]
    lane = lax.broadcasted_iota(jnp.int32, (SLICE, 128), 1)
    wide = None
    for y in range(NY):
        first = 3 * QUARTER
        blocks = [came[y, first + b * SLICE : first + (b + 1) * SLICE] for b in range(3)]
        blocks[2] = jnp.where(lane < SUB - 256, blocks[2], 0.0)
        row = jnp.concatenate(blocks + [jnp.zeros((SLICE, COLS - 384), f32)], axis=1)
        row = jnp.concatenate([row, jnp.zeros((16 - SLICE, COLS), f32)], axis=0)
        row = row if y == 0 else pltpu.roll(row, y * SUB, 1)
        wide = row if wide is None else wide + row
    passage_grad[...] = wide[:SLICE]


def merge(pairs):
    top, total = pairs[:, :8], pairs[:, 8:]
    peak = jnp.max(top, axis=0)
    return jnp.concatenate([peak, jnp.sum(total * jnp.exp(top - peak[None]), axis=0)])


def around(x, axis, n, step):
    return lax.ppermute(x, axis, [(i, (i + step) % n) for i in range(n)])


def body(queries, passages, positive):
    place = jnp.asarray(placement(), bf16)
    where = jnp.stack([lax.axis_index("core"), lax.axis_index("x")]).astype(jnp.int32)

    (message,) = call(
        prep_kernel,
        [shape(bf16, NY, MSG, 128)],
        queries,
        positive[None],
        passages.T,
        far=(0, 1, 2),
        scratch=[
            pltpu.VMEM((ROWS, WIDTH), bf16),
            pltpu.VMEM((1, ROWS), jnp.int32),
            pltpu.VMEM((SLICE, COLS), bf16),
            pltpu.VMEM((ROWS, 128), f32),
            pltpu.VMEM((16, COLS), f32),
            pltpu.SemaphoreType.DMA((3,)),
        ],
    )
    message = lax.all_to_all(message, "y", 0, 0, tiled=True)
    parts, passage_part = call(
        split_kernel,
        [shape(bf16, NX * NC, TALL, 128), shape(bf16, 112, 128)],
        message,
        far_outs=(0,),
        scratch=[pltpu.VMEM((NY * SLICE, 384), f32), pltpu.SemaphoreType.DMA((NY * NX * NC,))],
    )
    parts = lax.all_to_all(parts, ("core", "x"), 0, 0, tiled=True)
    passage_part = lax.all_gather(passage_part, "z")

    passage_part, row_pairs, col_pairs, placed, targets = call(
        tile_kernel,
        [
            shape(bf16, NC * THIRD, SUB),
            shape(f32, NX * NC, 16, 128),
            shape(f32, NZ, 8, 128),
            shape(bf16, TALL, NC * THIRD),
            shape(f32, 8, 128),
        ],
        parts,
        passage_part,
        place,
        scratch=[
            pltpu.VMEM((TALL, HALF), bf16),
            pltpu.VMEM((TALL, SUB), f32),
            pltpu.VMEM((NC * THIRD, 128), f32),
            pltpu.VMEM((16, 128), f32),
            pltpu.VMEM((8, 128), f32),
            pltpu.SemaphoreType.DMA((NX * NC + NZ,)),
        ],
        far_outs=(1, 2),
        flops=2 * TALL * SUB * NC * HALF,
    )
    own_half, other_half = call(
        spread_kernel,
        [shape(bf16, HALF, SUB)] * 2,
        where,
        passage_part,
        place,
        flops=2 * NC * HALF * THIRD * SUB,
    )
    other_half = around(other_half, "core", NC, 1)
    col_pairs, own_half = lax.optimization_barrier((col_pairs, own_half))
    targets, other_half = lax.optimization_barrier((targets, other_half))
    row_pairs = lax.all_to_all(row_pairs, ("x", "core"), 0, 0, tiled=True)
    col_pairs = lax.all_to_all(col_pairs, "z", 0, 0, tiled=True)
    row_pairs = lax.all_gather(merge(row_pairs), "y")

    block = (lax.axis_index("x") * NC + lax.axis_index("core")) * NY + lax.axis_index("y")
    ids = (block * SUB + jnp.arange(SUB, dtype=jnp.int32)).astype(f32)[None]
    dlogits, terms = call(
        passage_kernel,
        [shape(bf16, TALL, 384), shape(bf16, NZ, 112, 128)],
        placed,
        passage_part,
        targets,
        ids,
        row_pairs,
        col_pairs,
        far_outs=(1,),
        scratch=[
            pltpu.VMEM((NY, 4 * NY * SLICE, 128), f32),
            pltpu.VMEM((NZ, 112, 128), bf16),
            pltpu.SemaphoreType.DMA((NZ // 4,)),
        ],
        flops=2 * TALL * SUB * NC * THIRD,
    )
    terms = lax.all_to_all(terms, "z", 0, 0, tiled=True)

    own, *others = call(
        query_kernel,
        [shape(f32, 3 * ROWS, 128)] + [shape(bf16, 3 * ROWS, 128)] * (NX - 1),
        where,
        dlogits,
        around(dlogits, "core", NC, 1),
        own_half,
        other_half,
        scratch=[pltpu.VMEM((TALL, HALF), f32)],
        flops=4 * TALL * SUB * HALF,
    )
    came = [around(other, "x", NX, step) for step, other in enumerate(others, 1)]

    (message,) = call(
        fold_kernel,
        [shape(f32, NY, ROWS, 128)],
        terms,
        own,
        *came,
        scratch=[pltpu.VMEM((112, 128), f32), pltpu.VMEM((ROWS, 128), f32)],
    )
    message = lax.all_to_all(message, "y", 0, 0, tiled=True)
    query_grad, passage_grad = call(
        final_kernel,
        [shape(f32, ROWS, WIDTH), shape(f32, SLICE, COLS)],
        message,
        scratch=[pltpu.VMEM((3 * QUARTER, 128), f32)],
    )
    return (query_grad, passage_grad.T)


def solution(mesh):
    chips = Mesh(mesh.devices.reshape(NY, NZ, NX, NC), ("y", "z", "x", "core"))
    yz, xc = ("y", "z"), ("x", "core")
    return jax.shard_map(
        body,
        mesh=chips,
        in_specs=(P(yz, xc), P(xc, yz), P(yz)),
        out_specs=(P(yz, xc), P(xc, yz)),
        check_vma=False,
    )
```

```python
import jax
import jax.numpy as jnp
import numpy as np
from jax import lax
from jax.experimental import pallas as pl
from jax.experimental.pallas import tpu as pltpu
from jax.sharding import Mesh, PartitionSpec as P

logit_scale = 20.0
f32 = jnp.float32
bf16 = jnp.bfloat16
NY, NZ, NX, NC = 4, 16, 4, 2
ROWS, WIDTH = 144, 96
COLS, SLICE = 1152, 12
TALL, SUB = NY * ROWS, COLS // NY
HALF = NX * 128
THIRD = NZ * NY * SLICE // NC
BLOCKS = [(0, 128), (128, 128), (256, 128), (384, 128), (512, 64)]
MSG = ROWS + 48
QUARTER = ROWS // 4
GROUP = 384
NT = (((1,), (1,)), ((), ()))
TN = (((0,), (0,)), ((), ()))


def call(kernel, outs, *args, far=(), far_outs=(), scratch=(), flops=0):
    bytes_accessed = sum(int(np.prod(a.shape)) * a.dtype.itemsize for a in (*args, *outs))
    vmem, smem, hbm = (pl.BlockSpec(memory_space=m) for m in (pltpu.VMEM, pltpu.SMEM, pltpu.HBM))
    return pl.pallas_call(
        kernel,
        out_shape=[pltpu.HBM(o.shape, o.dtype) if i in far_outs else o for i, o in enumerate(outs)],
        in_specs=[hbm if i in far else smem if a.ndim == 1 else vmem for i, a in enumerate(args)],
        out_specs=[hbm if i in far_outs else vmem for i in range(len(outs))],
        scratch_shapes=list(scratch),
        compiler_params=pltpu.CompilerParams(vmem_limit_bytes=32 << 20),
        cost_estimate=pl.CostEstimate(flops=flops, bytes_accessed=bytes_accessed, transcendentals=0),
    )(*(pltpu.with_memory_space_constraint(a, pltpu.HBM) if i in far else a for i, a in enumerate(args)))


def shape(dtype, *dims):
    return jax.ShapeDtypeStruct(dims, dtype)


def placement():
    table = np.zeros((NX, 128, NZ // NC, NY, SLICE), np.float32)
    for x in range(NX):
        for lane in range(WIDTH):
            table[x, lane, lane // SLICE, x, lane % SLICE] = 1.0
    return table.reshape(HALF, THIRD)


def columns(wide, width):
    lane = lax.broadcasted_iota(jnp.int32, (128, 128), 1)
    packed = jnp.ones((128, 128), f32)
    for j, group in enumerate(wide):
        for g, column in enumerate(group):
            if column.shape[0] < 128:
                column = jnp.concatenate([column, jnp.ones((128 - column.shape[0], 1), f32)], axis=0)
            packed = jnp.where(lane == 8 * g + j, column, packed)
    return packed.T[:width]


def upright(lines):
    return jnp.concatenate([lines, jnp.zeros((120, 128), f32)], axis=0).T


def prep_kernel(queries_in, positive_in, passages_in, message, queries, positive, passages, wide, tall, sems):
    pairs = ((queries_in, queries), (positive_in, positive), (passages_in, passages))
    copies = [pltpu.make_async_copy(a, b, sems.at[i]) for i, (a, b) in enumerate(pairs)]
    for copy in copies:
        copy.start()
    for copy in copies:
        copy.wait()
    index = positive[...].astype(f32)
    index = jnp.concatenate(
        [index[:, :128], jnp.concatenate([index[:, 128:], jnp.zeros((1, 256 - ROWS), f32)], axis=1)], axis=0
    )
    index = upright(jnp.concatenate([index, jnp.zeros((6, 128), f32)], axis=0))
    index = jnp.concatenate([index[:, 0:1], index[: ROWS - 128, 1:2]], axis=0)
    high = jnp.floor(index * (1.0 / 128.0))
    low = index - 128.0 * high
    wide[...] = jnp.zeros((ROWS, 128), f32)
    wide[:, :WIDTH] = queries[...].astype(f32)
    lane = lax.broadcasted_iota(jnp.int32, (ROWS, 128), 1)
    own = jnp.where(lane == WIDTH, high, jnp.where(lane == WIDTH + 1, low, wide[...])).astype(bf16)
    tall[...] = jnp.zeros((16, COLS), f32)
    tall[:SLICE] = passages[...].astype(f32)
    for y in range(NY):
        message[y, :ROWS] = own
        piece = pltpu.roll(tall[...], (COLS - y * SUB) % COLS, 1)
        for b in range(3):
            message[y, ROWS + 16 * b : ROWS + 16 * b + 16] = piece[:, b * 128 : (b + 1) * 128].astype(bf16)


def split_kernel(came, queries, part, staged, total, sems):
    for y in range(NY):
        staged[y * ROWS : (y + 1) * ROWS] = came[y, :ROWS]
    copies = [pltpu.make_async_copy(staged, queries.at[i], sems.at[i]) for i in range(NX * NC)]
    for copy in copies:
        copy.start()
    for y in range(NY):
        for b in range(3):
            piece = came[y, ROWS + 16 * b : ROWS + 16 * b + 16].astype(f32)
            total[y * SLICE : (y + 1) * SLICE, b * 128 : (b + 1) * 128] = piece[:SLICE]
    high = NY * SLICE
    for b in range(2):
        part[b * high : (b + 1) * high] = total[:, b * 128 : (b + 1) * 128].astype(bf16)
    lane = lax.broadcasted_iota(jnp.int32, (SLICE, 128), 1)
    tail = jnp.zeros((SLICE, 128), f32)
    for y in range(NY):
        piece = jnp.where(lane < SUB - 256, total[y * SLICE : (y + 1) * SLICE, 256:], 0.0)
        tail += piece if y == 0 else pltpu.roll(piece, 32 * y, 1)
    tail = jnp.concatenate([tail, jnp.zeros((16 - SLICE, 128), f32)], axis=0)
    part[2 * high :] = tail.astype(bf16)
    for copy in copies:
        copy.wait()


def unpack(came, passages, tails):
    high = NY * SLICE
    for z in range(NZ):
        for b in range(2):
            passages[z * high : (z + 1) * high, b * 128 : (b + 1) * 128] = came[z, b * high : (b + 1) * high]
    packed = came[:, 2 * high :].astype(f32).reshape(NZ * 16, 128)
    for y in range(NY):
        moved = packed if y == 0 else pltpu.roll(packed, 128 - 32 * y, 1)
        for z in range(NZ):
            tails[z * high + y * SLICE : z * high + (y + 1) * SLICE] = moved[z * 16 : z * 16 + SLICE]
    passages[:, 256:] = tails[:, : SUB - 256].astype(bf16)


def tile_kernel(
    parts, came, place, passages, row_pairs, col_pairs, placed, targets, query_half, logits, tails, rows, cols, sems
):
    unpack(came, passages, tails)
    for c in range(NC):
        for x in range(NX):
            query_half[:, x * 128 : (x + 1) * 128] = parts[c * NX + x]
        placed[:, c * THIRD : (c + 1) * THIRD] = jnp.dot(
            query_half[...], place[...], preferred_element_type=f32
        ).astype(bf16)
    pairs, col_top = [], None
    for start, size in BLOCKS:
        scores = logit_scale * jnp.dot(
            placed[start : start + size], passages[...], preferred_element_type=f32
        )
        logits[start : start + size] = scores
        top = jnp.max(scores, axis=1, keepdims=True)
        pairs.append((top, jnp.sum(jnp.exp(scores - top), axis=1, keepdims=True)))
        peak = jnp.max(scores, axis=0, keepdims=True)
        col_top = peak if col_top is None else jnp.maximum(col_top, peak)
    rows[...] = columns(pairs, 16)
    copies = [pltpu.make_async_copy(rows, row_pairs.at[i], sems.at[i]) for i in range(NX * NC)]
    for copy in copies:
        copy.start()
    col_sum = jnp.zeros((1, SUB), f32)
    for start, size in BLOCKS:
        col_sum += jnp.sum(jnp.exp(logits[start : start + size] - col_top), axis=0, keepdims=True)
    fill = jnp.ones((1, 384 - SUB), f32)
    both = [jnp.concatenate([v, fill], axis=1) for v in (col_top, col_sum)]
    lines = [v[:, b * 128 : (b + 1) * 128] for v in both for b in range(3)]
    cols[...] = jnp.concatenate(lines + [jnp.ones((2, 128), f32)], axis=0)
    for i in range(NZ):
        copies.append(pltpu.make_async_copy(cols, col_pairs.at[i], sems.at[NX * NC + i]))
        copies[-1].start()
    spare = parts[0].astype(f32)
    target = spare[:, WIDTH : WIDTH + 1] * 128.0 + spare[:, WIDTH + 1 : WIDTH + 2]
    targets[...] = columns([(target[start : start + size],) for start, size in BLOCKS], 8)
    for copy in copies:
        copy.wait()


def spread_kernel(where, passages, place, own_half, other_half):
    for c, half in ((where[0], own_half), (1 - where[0], other_half)):
        rows = pl.ds(pl.multiple_of(c * THIRD, THIRD), THIRD)
        half[...] = jnp.dot(place[...], passages[rows], preferred_element_type=f32).astype(bf16)


def passage_kernel(placed, passages, targets, ids, row_pairs, col_pairs, dlogits, out, tails, terms, sems):
    top, total = row_pairs[:, :8], row_pairs[:, 8:]
    peak = jnp.max(top, axis=0)
    row_lse = upright(peak + jnp.log(jnp.sum(total * jnp.exp(top - peak[None]), axis=0)))
    target = upright(targets[...])
    pairs = col_pairs[...]
    top, total = pairs[:, 0:3], pairs[:, 3:6]
    peak = jnp.max(top, axis=0)
    col_lse = peak + jnp.log(jnp.sum(total * jnp.exp(top - peak[None]), axis=0))
    col_lse = jnp.concatenate([col_lse[b : b + 1] for b in range(3)], axis=1)[:, :SUB]
    dlogits[:, 256:] = jnp.zeros((TALL, 128), bf16)
    for j, (start, size) in enumerate(BLOCKS):
        scores = logit_scale * jnp.dot(placed[start : start + size], passages[...], preferred_element_type=f32)
        slope = jnp.exp(scores - row_lse[:size, j : j + 1]) + jnp.exp(scores - col_lse)
        hit = jnp.where(target[:size, j : j + 1] == ids[...], 2.0, 0.0)
        dlogits[start : start + size, :SUB] = (slope - hit).astype(bf16)
    high = NY * SLICE
    copies = []
    for first in range(0, NZ, 4):
        if first * high % GROUP == 0:
            whole = logit_scale * lax.dot_general(
                placed[:, first * high : first * high + GROUP], dlogits[...], TN, preferred_element_type=f32
            )
        offset = first * high % GROUP
        part = whole[offset : offset + 4 * high]
        tails[...] = part[:, 256:]
        for i in range(4):
            for b in range(2):
                piece = part[i * high : (i + 1) * high, b * 128 : (b + 1) * 128]
                terms[first + i, b * high : (b + 1) * high] = piece.astype(bf16)
            tail = jnp.zeros((16, 128), f32)
            for a in range(NY):
                first_row = i * high + a * SLICE
                piece = jnp.concatenate([tails[first_row : first_row + SLICE], jnp.zeros((16 - SLICE, 128), f32)], axis=0)
                tail += piece if a == 0 else pltpu.roll(piece, 32 * a, 1)
            terms[first + i, 2 * high : 2 * high + 16] = tail.astype(bf16)
        group = pl.ds(first, 4)
        copies.append(pltpu.make_async_copy(terms.at[group], out.at[group], sems.at[first // 4]))
        copies[-1].start()
    for copy in copies:
        copy.wait()


def squeeze(block):
    lane = lax.broadcasted_iota(jnp.int32, (ROWS, 128), 1)
    tail = block[3 * ROWS :]
    parts = []
    for j in range(3):
        moved = pltpu.roll(tail, WIDTH - 32 * j, 1)
        parts.append(jnp.where(lane < WIDTH, block[j * ROWS : (j + 1) * ROWS], moved))
    return jnp.concatenate(parts, axis=0)


def query_kernel(where, dlogits, other_dlogits, own_half, other_half, own, *rest):
    outs, total = rest[:-1], rest[-1]
    total[...] = logit_scale * (
        lax.dot_general(dlogits[:, :SUB], own_half[...], NT, preferred_element_type=f32)
        + lax.dot_general(other_dlogits[:, :SUB], other_half[...], NT, preferred_element_type=f32)
    )
    own[...] = squeeze(total[:, pl.ds(pl.multiple_of(where[1] * 128, 128), 128)])
    for step, out in enumerate(outs, 1):
        lanes = pl.ds(pl.multiple_of(lax.rem(where[1] + step, NX) * 128, 128), 128)
        out[...] = squeeze(total[:, lanes]).astype(bf16)


def fold_kernel(terms, own, *rest):
    came, message, total, block = rest[:-3], rest[-3], rest[-2], rest[-1]
    high = NY * SLICE
    total[...] = jnp.sum(terms[...].astype(f32), axis=0)
    lane = lax.broadcasted_iota(jnp.int32, (ROWS, 128), 1)
    short = lax.broadcasted_iota(jnp.int32, (QUARTER, 128), 1)
    last = jnp.zeros((ROWS, 128), f32)
    for y in range(NY):
        if y < 3:
            rows = slice(y * ROWS, (y + 1) * ROWS)
            value = own[rows] + sum(c[rows].astype(f32) for c in came)
            moved = pltpu.roll(value, (128 + 32 * y - WIDTH) % 128, 1)
            last = jnp.where((lane >= 32 * y) & (lane < 32 * y + 32), moved, last)
        else:
            value = last
        block[...] = value
        extra = block[3 * QUARTER :]
        for j in range(3):
            moved = pltpu.roll(extra, WIDTH - 32 * j, 1)
            piece = block[j * QUARTER : (j + 1) * QUARTER]
            message[y, j * QUARTER : (j + 1) * QUARTER] = jnp.where(short < WIDTH, piece, moved)
        tail = total[2 * high :]
        tail = tail if y == 0 else pltpu.roll(tail, 128 - 32 * y, 1)
        for b in range(3):
            piece = tail[:SLICE] if b == 2 else total[b * high + y * SLICE : b * high + (y + 1) * SLICE]
            message[y, 3 * QUARTER + b * SLICE : 3 * QUARTER + (b + 1) * SLICE] = piece


def final_kernel(came, query_grad, passage_grad, total):
    total[...] = jnp.sum(came[:, : 3 * QUARTER], axis=0)
    short = lax.broadcasted_iota(jnp.int32, (QUARTER, 128), 1)
    last = jnp.zeros((QUARTER, 128), f32)
    for j in range(3):
        rows = slice(j * QUARTER, (j + 1) * QUARTER)
        query_grad[rows] = total[rows, :WIDTH]
        moved = pltpu.roll(total[rows], (128 + 32 * j - WIDTH) % 128, 1)
        last = jnp.where((short >= 32 * j) & (short < 32 * j + 32), moved, last)
    query_grad[3 * QUARTER :] = last[:, :WIDTH]
    lane = lax.broadcasted_iota(jnp.int32, (SLICE, 128), 1)
    wide = None
    for y in range(NY):
        first = 3 * QUARTER
        blocks = [came[y, first + b * SLICE : first + (b + 1) * SLICE] for b in range(3)]
        blocks[2] = jnp.where(lane < SUB - 256, blocks[2], 0.0)
        row = jnp.concatenate(blocks + [jnp.zeros((SLICE, COLS - 384), f32)], axis=1)
        row = jnp.concatenate([row, jnp.zeros((16 - SLICE, COLS), f32)], axis=0)
        row = row if y == 0 else pltpu.roll(row, y * SUB, 1)
        wide = row if wide is None else wide + row
    passage_grad[...] = wide[:SLICE]


def merge(pairs):
    top, total = pairs[:, :8], pairs[:, 8:]
    peak = jnp.max(top, axis=0)
    return jnp.concatenate([peak, jnp.sum(total * jnp.exp(top - peak[None]), axis=0)])


def around(x, axis, n, step):
    return lax.ppermute(x, axis, [(i, (i + step) % n) for i in range(n)])


def body(queries, passages, positive):
    place = jnp.asarray(placement(), bf16)
    where = jnp.stack([lax.axis_index("core"), lax.axis_index("x")]).astype(jnp.int32)

    (message,) = call(
        prep_kernel,
        [shape(bf16, NY, MSG, 128)],
        queries,
        positive[None],
        passages.T,
        far=(0, 1, 2),
        scratch=[
            pltpu.VMEM((ROWS, WIDTH), bf16),
            pltpu.VMEM((1, ROWS), jnp.int32),
            pltpu.VMEM((SLICE, COLS), bf16),
            pltpu.VMEM((ROWS, 128), f32),
            pltpu.VMEM((16, COLS), f32),
            pltpu.SemaphoreType.DMA((3,)),
        ],
    )
    message = lax.all_to_all(message, "y", 0, 0, tiled=True)
    parts, passage_part = call(
        split_kernel,
        [shape(bf16, NX * NC, TALL, 128), shape(bf16, 112, 128)],
        message,
        far_outs=(0,),
        scratch=[
            pltpu.VMEM((TALL, 128), bf16),
            pltpu.VMEM((NY * SLICE, 384), f32),
            pltpu.SemaphoreType.DMA((NX * NC,)),
        ],
    )
    parts = lax.all_to_all(parts, ("core", "x"), 0, 0, tiled=True)
    passage_part = lax.all_gather(passage_part, "z")

    passage_part, row_pairs, col_pairs, placed, targets = call(
        tile_kernel,
        [
            shape(bf16, NC * THIRD, SUB),
            shape(f32, NX * NC, 16, 128),
            shape(f32, NZ, 8, 128),
            shape(bf16, TALL, NC * THIRD),
            shape(f32, 8, 128),
        ],
        parts,
        passage_part,
        place,
        scratch=[
            pltpu.VMEM((TALL, HALF), bf16),
            pltpu.VMEM((TALL, SUB), f32),
            pltpu.VMEM((NC * THIRD, 128), f32),
            pltpu.VMEM((16, 128), f32),
            pltpu.VMEM((8, 128), f32),
            pltpu.SemaphoreType.DMA((NX * NC + NZ,)),
        ],
        far_outs=(1, 2),
        flops=2 * TALL * SUB * NC * HALF,
    )
    own_half, other_half = call(
        spread_kernel,
        [shape(bf16, HALF, SUB)] * 2,
        where,
        passage_part,
        place,
        flops=2 * NC * HALF * THIRD * SUB,
    )
    other_half = around(other_half, "core", NC, 1)
    col_pairs, own_half = lax.optimization_barrier((col_pairs, own_half))
    targets, other_half = lax.optimization_barrier((targets, other_half))
    row_pairs = lax.all_to_all(row_pairs, ("x", "core"), 0, 0, tiled=True)
    col_pairs = lax.all_to_all(col_pairs, "z", 0, 0, tiled=True)
    row_pairs = lax.all_gather(merge(row_pairs), "y")

    block = (lax.axis_index("x") * NC + lax.axis_index("core")) * NY + lax.axis_index("y")
    ids = (block * SUB + jnp.arange(SUB, dtype=jnp.int32)).astype(f32)[None]
    dlogits, terms = call(
        passage_kernel,
        [shape(bf16, TALL, 384), shape(bf16, NZ, 112, 128)],
        placed,
        passage_part,
        targets,
        ids,
        row_pairs,
        col_pairs,
        far_outs=(1,),
        scratch=[
            pltpu.VMEM((4 * NY * SLICE, 128), f32),
            pltpu.VMEM((NZ, 112, 128), bf16),
            pltpu.SemaphoreType.DMA((NZ // 4,)),
        ],
        flops=2 * TALL * SUB * NC * THIRD,
    )
    terms = lax.all_to_all(terms, "z", 0, 0, tiled=True)

    own, *others = call(
        query_kernel,
        [shape(f32, 3 * ROWS, 128)] + [shape(bf16, 3 * ROWS, 128)] * (NX - 1),
        where,
        dlogits,
        around(dlogits, "core", NC, 1),
        own_half,
        other_half,
        scratch=[pltpu.VMEM((TALL, HALF), f32)],
        flops=4 * TALL * SUB * HALF,
    )
    came = [around(other, "x", NX, step) for step, other in enumerate(others, 1)]

    (message,) = call(
        fold_kernel,
        [shape(f32, NY, ROWS, 128)],
        terms,
        own,
        *came,
        scratch=[pltpu.VMEM((112, 128), f32), pltpu.VMEM((ROWS, 128), f32)],
    )
    message = lax.all_to_all(message, "y", 0, 0, tiled=True)
    query_grad, passage_grad = call(
        final_kernel,
        [shape(f32, ROWS, WIDTH), shape(f32, SLICE, COLS)],
        message,
        scratch=[pltpu.VMEM((3 * QUARTER, 128), f32)],
    )
    return (query_grad, passage_grad.T)


def solution(mesh):
    chips = Mesh(mesh.devices.reshape(NY, NZ, NX, NC), ("y", "z", "x", "core"))
    yz, xc = ("y", "z"), ("x", "core")
    return jax.shard_map(
        body,
        mesh=chips,
        in_specs=(P(yz, xc), P(xc, yz), P(yz)),
        out_specs=(P(yz, xc), P(xc, yz)),
        check_vma=False,
    )
```

```python
import jax
import jax.numpy as jnp
import numpy as np
from jax import lax
from jax.experimental import pallas as pl
from jax.experimental.pallas import tpu as pltpu
from jax.sharding import Mesh, PartitionSpec as P

logit_scale = 20.0
f32 = jnp.float32
bf16 = jnp.bfloat16
NY, NZ, NX, NC = 4, 16, 4, 2
ROWS, WIDTH = 144, 96
COLS, SLICE = 1152, 12
TALL, SUB = NY * ROWS, COLS // NY
HALF = NX * 128
THIRD = NZ * NY * SLICE // NC
BLOCKS = [(0, 128), (128, 128), (256, 128), (384, 128), (512, 64)]
MSG = ROWS + 48
QUARTER = ROWS // 4
GROUP = 384
NT = (((1,), (1,)), ((), ()))
TN = (((0,), (0,)), ((), ()))


def call(kernel, outs, *args, far=(), far_outs=(), scratch=(), flops=0):
    bytes_accessed = sum(int(np.prod(a.shape)) * a.dtype.itemsize for a in (*args, *outs))
    vmem, smem, hbm = (pl.BlockSpec(memory_space=m) for m in (pltpu.VMEM, pltpu.SMEM, pltpu.HBM))
    return pl.pallas_call(
        kernel,
        out_shape=[pltpu.HBM(o.shape, o.dtype) if i in far_outs else o for i, o in enumerate(outs)],
        in_specs=[hbm if i in far else smem if a.ndim == 1 else vmem for i, a in enumerate(args)],
        out_specs=[hbm if i in far_outs else vmem for i in range(len(outs))],
        scratch_shapes=list(scratch),
        compiler_params=pltpu.CompilerParams(vmem_limit_bytes=32 << 20),
        cost_estimate=pl.CostEstimate(flops=flops, bytes_accessed=bytes_accessed, transcendentals=0),
    )(*(pltpu.with_memory_space_constraint(a, pltpu.HBM) if i in far else a for i, a in enumerate(args)))


def shape(dtype, *dims):
    return jax.ShapeDtypeStruct(dims, dtype)


def placement():
    table = np.zeros((NX, 128, NZ // NC, NY, SLICE), np.float32)
    for x in range(NX):
        for lane in range(WIDTH):
            table[x, lane, lane // SLICE, x, lane % SLICE] = 1.0
    return table.reshape(HALF, THIRD)


def columns(wide, width):
    lane = lax.broadcasted_iota(jnp.int32, (128, 128), 1)
    packed = jnp.ones((128, 128), f32)
    for j, group in enumerate(wide):
        for g, column in enumerate(group):
            if column.shape[0] < 128:
                column = jnp.concatenate([column, jnp.ones((128 - column.shape[0], 1), f32)], axis=0)
            packed = jnp.where(lane == 8 * g + j, column, packed)
    return packed.T[:width]


def upright(lines):
    return jnp.concatenate([lines, jnp.zeros((120, 128), f32)], axis=0).T


def prep_kernel(queries_in, positive_in, passages_in, message, queries, positive, passages, wide, tall, sems):
    pairs = ((queries_in, queries), (positive_in, positive), (passages_in, passages))
    copies = [pltpu.make_async_copy(a, b, sems.at[i]) for i, (a, b) in enumerate(pairs)]
    for copy in copies:
        copy.start()
    for copy in copies:
        copy.wait()
    index = positive[...].astype(f32)
    index = jnp.concatenate(
        [index[:, :128], jnp.concatenate([index[:, 128:], jnp.zeros((1, 256 - ROWS), f32)], axis=1)], axis=0
    )
    index = upright(jnp.concatenate([index, jnp.zeros((6, 128), f32)], axis=0))
    index = jnp.concatenate([index[:, 0:1], index[: ROWS - 128, 1:2]], axis=0)
    high = jnp.floor(index * (1.0 / 128.0))
    low = index - 128.0 * high
    wide[...] = jnp.zeros((ROWS, 128), f32)
    wide[:, :WIDTH] = queries[...].astype(f32)
    lane = lax.broadcasted_iota(jnp.int32, (ROWS, 128), 1)
    own = jnp.where(lane == WIDTH, high, jnp.where(lane == WIDTH + 1, low, wide[...])).astype(bf16)
    tall[...] = jnp.zeros((16, COLS), f32)
    tall[:SLICE] = passages[...].astype(f32)
    for y in range(NY):
        message[y, :ROWS] = own
        piece = pltpu.roll(tall[...], (COLS - y * SUB) % COLS, 1)
        for b in range(3):
            message[y, ROWS + 16 * b : ROWS + 16 * b + 16] = piece[:, b * 128 : (b + 1) * 128].astype(bf16)


def split_kernel(came, queries, part, staged, total, sems):
    for y in range(NY):
        staged[y * ROWS : (y + 1) * ROWS] = came[y, :ROWS]
    copies = [pltpu.make_async_copy(staged, queries.at[i], sems.at[i]) for i in range(NX * NC)]
    for copy in copies:
        copy.start()
    for y in range(NY):
        for b in range(3):
            piece = came[y, ROWS + 16 * b : ROWS + 16 * b + 16].astype(f32)
            total[y * SLICE : (y + 1) * SLICE, b * 128 : (b + 1) * 128] = piece[:SLICE]
    high = NY * SLICE
    for b in range(2):
        part[b * high : (b + 1) * high] = total[:, b * 128 : (b + 1) * 128].astype(bf16)
    lane = lax.broadcasted_iota(jnp.int32, (SLICE, 128), 1)
    tail = jnp.zeros((SLICE, 128), f32)
    for y in range(NY):
        piece = jnp.where(lane < SUB - 256, total[y * SLICE : (y + 1) * SLICE, 256:], 0.0)
        tail += piece if y == 0 else pltpu.roll(piece, 32 * y, 1)
    tail = jnp.concatenate([tail, jnp.zeros((16 - SLICE, 128), f32)], axis=0)
    part[2 * high :] = tail.astype(bf16)
    for copy in copies:
        copy.wait()


def unpack(came, passages, tails):
    high = NY * SLICE
    for z in range(NZ):
        for b in range(2):
            passages[z * high : (z + 1) * high, b * 128 : (b + 1) * 128] = came[z, b * high : (b + 1) * high]
    packed = came[:, 2 * high :].astype(f32).reshape(NZ * 16, 128)
    for y in range(NY):
        moved = packed if y == 0 else pltpu.roll(packed, 128 - 32 * y, 1)
        for z in range(NZ):
            tails[z * high + y * SLICE : z * high + (y + 1) * SLICE] = moved[z * 16 : z * 16 + SLICE]
    passages[:, 256:] = tails[:, : SUB - 256].astype(bf16)


def tile_kernel(
    parts, came, place, passages, row_pairs, col_pairs, placed, targets, query_half, logits, tails, cols, sems
):
    unpack(came, passages, tails)
    for c in range(NC):
        for x in range(NX):
            query_half[:, x * 128 : (x + 1) * 128] = parts[c * NX + x]
        placed[:, c * THIRD : (c + 1) * THIRD] = jnp.dot(
            query_half[...], place[...], preferred_element_type=f32
        ).astype(bf16)
    pairs, col_top = [], None
    for start, size in BLOCKS:
        scores = logit_scale * jnp.dot(
            placed[start : start + size], passages[...], preferred_element_type=f32
        )
        logits[start : start + size] = scores
        top = jnp.max(scores, axis=1, keepdims=True)
        pairs.append((top, jnp.sum(jnp.exp(scores - top), axis=1, keepdims=True)))
        peak = jnp.max(scores, axis=0, keepdims=True)
        col_top = peak if col_top is None else jnp.maximum(col_top, peak)
    row_pairs[...] = columns(pairs, 16)
    col_sum = jnp.zeros((1, SUB), f32)
    for start, size in BLOCKS:
        col_sum += jnp.sum(jnp.exp(logits[start : start + size] - col_top), axis=0, keepdims=True)
    fill = jnp.ones((1, 384 - SUB), f32)
    both = [jnp.concatenate([v, fill], axis=1) for v in (col_top, col_sum)]
    lines = [v[:, b * 128 : (b + 1) * 128] for v in both for b in range(3)]
    cols[...] = jnp.concatenate(lines + [jnp.ones((2, 128), f32)], axis=0)
    copies = [pltpu.make_async_copy(cols, col_pairs.at[i], sems.at[i]) for i in range(NZ)]
    for copy in copies:
        copy.start()
    spare = parts[0].astype(f32)
    target = spare[:, WIDTH : WIDTH + 1] * 128.0 + spare[:, WIDTH + 1 : WIDTH + 2]
    targets[...] = columns([(target[start : start + size],) for start, size in BLOCKS], 8)
    for copy in copies:
        copy.wait()


def spread_kernel(where, passages, place, own_half, other_out, other_half, sem):
    for c, half in ((1 - where[0], other_half), (where[0], own_half)):
        rows = pl.ds(pl.multiple_of(c * THIRD, THIRD), THIRD)
        half[...] = jnp.dot(place[...], passages[rows], preferred_element_type=f32).astype(bf16)
        if half is other_half:
            copy = pltpu.make_async_copy(other_half, other_out, sem)
            copy.start()
    copy.wait()


def passage_kernel(placed, passages, targets, ids, row_pairs, col_pairs, dlogits, out, tails, terms, sems):
    top, total = row_pairs[:, :8], row_pairs[:, 8:]
    peak = jnp.max(top, axis=0)
    row_lse = upright(peak + jnp.log(jnp.sum(total * jnp.exp(top - peak[None]), axis=0)))
    target = upright(targets[...])
    pairs = col_pairs[...]
    top, total = pairs[:, 0:3], pairs[:, 3:6]
    peak = jnp.max(top, axis=0)
    col_lse = peak + jnp.log(jnp.sum(total * jnp.exp(top - peak[None]), axis=0))
    col_lse = jnp.concatenate([col_lse[b : b + 1] for b in range(3)], axis=1)[:, :SUB]
    dlogits[:, 256:] = jnp.zeros((TALL, 128), bf16)
    for j, (start, size) in enumerate(BLOCKS):
        scores = logit_scale * jnp.dot(placed[start : start + size], passages[...], preferred_element_type=f32)
        slope = jnp.exp(scores - row_lse[:size, j : j + 1]) + jnp.exp(scores - col_lse)
        hit = jnp.where(target[:size, j : j + 1] == ids[...], 2.0, 0.0)
        dlogits[start : start + size, :SUB] = (slope - hit).astype(bf16)
    high = NY * SLICE
    copies = []
    for first in range(0, NZ, 4):
        if first * high % GROUP == 0:
            whole = logit_scale * lax.dot_general(
                placed[:, first * high : first * high + GROUP], dlogits[...], TN, preferred_element_type=f32
            )
        offset = first * high % GROUP
        part = whole[offset : offset + 4 * high]
        tails[...] = part[:, 256:]
        for i in range(4):
            for b in range(2):
                piece = part[i * high : (i + 1) * high, b * 128 : (b + 1) * 128]
                terms[first + i, b * high : (b + 1) * high] = piece.astype(bf16)
            tail = jnp.zeros((16, 128), f32)
            for a in range(NY):
                first_row = i * high + a * SLICE
                piece = jnp.concatenate([tails[first_row : first_row + SLICE], jnp.zeros((16 - SLICE, 128), f32)], axis=0)
                tail += piece if a == 0 else pltpu.roll(piece, 32 * a, 1)
            terms[first + i, 2 * high : 2 * high + 16] = tail.astype(bf16)
        group = pl.ds(first, 4)
        copies.append(pltpu.make_async_copy(terms.at[group], out.at[group], sems.at[first // 4]))
        copies[-1].start()
    for copy in copies:
        copy.wait()


def squeeze(block):
    lane = lax.broadcasted_iota(jnp.int32, (ROWS, 128), 1)
    tail = block[3 * ROWS :]
    parts = []
    for j in range(3):
        moved = pltpu.roll(tail, WIDTH - 32 * j, 1)
        parts.append(jnp.where(lane < WIDTH, block[j * ROWS : (j + 1) * ROWS], moved))
    return jnp.concatenate(parts, axis=0)


def query_kernel(where, dlogits, other_dlogits, own_half, other_half, own, *rest):
    outs, total = rest[:-1], rest[-1]
    total[...] = logit_scale * (
        lax.dot_general(dlogits[:, :SUB], own_half[...], NT, preferred_element_type=f32)
        + lax.dot_general(other_dlogits[:, :SUB], other_half[...], NT, preferred_element_type=f32)
    )
    own[...] = squeeze(total[:, pl.ds(pl.multiple_of(where[1] * 128, 128), 128)])
    for step, out in enumerate(outs, 1):
        lanes = pl.ds(pl.multiple_of(lax.rem(where[1] + step, NX) * 128, 128), 128)
        out[...] = squeeze(total[:, lanes]).astype(bf16)


def fold_kernel(terms, own, *rest):
    came, message, total, block = rest[:-3], rest[-3], rest[-2], rest[-1]
    high = NY * SLICE
    total[...] = jnp.sum(terms[...].astype(f32), axis=0)
    lane = lax.broadcasted_iota(jnp.int32, (ROWS, 128), 1)
    short = lax.broadcasted_iota(jnp.int32, (QUARTER, 128), 1)
    last = jnp.zeros((ROWS, 128), f32)
    for y in range(NY):
        if y < 3:
            rows = slice(y * ROWS, (y + 1) * ROWS)
            value = own[rows] + sum(c[rows].astype(f32) for c in came)
            moved = pltpu.roll(value, (128 + 32 * y - WIDTH) % 128, 1)
            last = jnp.where((lane >= 32 * y) & (lane < 32 * y + 32), moved, last)
        else:
            value = last
        block[...] = value
        extra = block[3 * QUARTER :]
        for j in range(3):
            moved = pltpu.roll(extra, WIDTH - 32 * j, 1)
            piece = block[j * QUARTER : (j + 1) * QUARTER]
            message[y, j * QUARTER : (j + 1) * QUARTER] = jnp.where(short < WIDTH, piece, moved)
        tail = total[2 * high :]
        tail = tail if y == 0 else pltpu.roll(tail, 128 - 32 * y, 1)
        for b in range(3):
            piece = tail[:SLICE] if b == 2 else total[b * high + y * SLICE : b * high + (y + 1) * SLICE]
            message[y, 3 * QUARTER + b * SLICE : 3 * QUARTER + (b + 1) * SLICE] = piece


def final_kernel(came, query_grad, passage_grad, total):
    total[...] = jnp.sum(came[:, : 3 * QUARTER], axis=0)
    short = lax.broadcasted_iota(jnp.int32, (QUARTER, 128), 1)
    last = jnp.zeros((QUARTER, 128), f32)
    for j in range(3):
        rows = slice(j * QUARTER, (j + 1) * QUARTER)
        query_grad[rows] = total[rows, :WIDTH]
        moved = pltpu.roll(total[rows], (128 + 32 * j - WIDTH) % 128, 1)
        last = jnp.where((short >= 32 * j) & (short < 32 * j + 32), moved, last)
    query_grad[3 * QUARTER :] = last[:, :WIDTH]
    lane = lax.broadcasted_iota(jnp.int32, (SLICE, 128), 1)
    wide = None
    for y in range(NY):
        first = 3 * QUARTER
        blocks = [came[y, first + b * SLICE : first + (b + 1) * SLICE] for b in range(3)]
        blocks[2] = jnp.where(lane < SUB - 256, blocks[2], 0.0)
        row = jnp.concatenate(blocks + [jnp.zeros((SLICE, COLS - 384), f32)], axis=1)
        row = jnp.concatenate([row, jnp.zeros((16 - SLICE, COLS), f32)], axis=0)
        row = row if y == 0 else pltpu.roll(row, y * SUB, 1)
        wide = row if wide is None else wide + row
    passage_grad[...] = wide[:SLICE]


def merge(pairs):
    top, total = pairs[:, :8], pairs[:, 8:]
    peak = jnp.max(top, axis=0)
    return jnp.concatenate([peak, jnp.sum(total * jnp.exp(top - peak[None]), axis=0)])


def around(x, axis, n, step):
    return lax.ppermute(x, axis, [(i, (i + step) % n) for i in range(n)])


def body(queries, passages, positive):
    place = jnp.asarray(placement(), bf16)
    where = jnp.stack([lax.axis_index("core"), lax.axis_index("x")]).astype(jnp.int32)

    (message,) = call(
        prep_kernel,
        [shape(bf16, NY, MSG, 128)],
        queries,
        positive[None],
        passages.T,
        far=(0, 1, 2),
        scratch=[
            pltpu.VMEM((ROWS, WIDTH), bf16),
            pltpu.VMEM((1, ROWS), jnp.int32),
            pltpu.VMEM((SLICE, COLS), bf16),
            pltpu.VMEM((ROWS, 128), f32),
            pltpu.VMEM((16, COLS), f32),
            pltpu.SemaphoreType.DMA((3,)),
        ],
    )
    message = lax.all_to_all(message, "y", 0, 0, tiled=True)
    parts, passage_part = call(
        split_kernel,
        [shape(bf16, NX * NC, TALL, 128), shape(bf16, 112, 128)],
        message,
        far_outs=(0,),
        scratch=[
            pltpu.VMEM((TALL, 128), bf16),
            pltpu.VMEM((NY * SLICE, 384), f32),
            pltpu.SemaphoreType.DMA((NX * NC,)),
        ],
    )
    parts = lax.all_to_all(parts, ("core", "x"), 0, 0, tiled=True)
    passage_part = lax.all_gather(passage_part, "z")

    passage_part, row_pairs, col_pairs, placed, targets = call(
        tile_kernel,
        [
            shape(bf16, NC * THIRD, SUB),
            shape(f32, 16, 128),
            shape(f32, NZ, 8, 128),
            shape(bf16, TALL, NC * THIRD),
            shape(f32, 8, 128),
        ],
        parts,
        passage_part,
        place,
        scratch=[
            pltpu.VMEM((TALL, HALF), bf16),
            pltpu.VMEM((TALL, SUB), f32),
            pltpu.VMEM((NC * THIRD, 128), f32),
            pltpu.VMEM((8, 128), f32),
            pltpu.SemaphoreType.DMA((NZ,)),
        ],
        far_outs=(2,),
        flops=2 * TALL * SUB * NC * HALF,
    )
    col_pairs = lax.all_to_all(col_pairs, "z", 0, 0, tiled=True)
    own_half, other_half = call(
        spread_kernel,
        [shape(bf16, HALF, SUB)] * 2,
        where,
        passage_part,
        place,
        far_outs=(1,),
        scratch=[pltpu.VMEM((HALF, SUB), bf16), pltpu.SemaphoreType.DMA],
        flops=2 * NC * HALF * THIRD * SUB,
    )
    row_pairs, own_half = lax.optimization_barrier((row_pairs, own_half))
    row_pairs = merge(lax.all_gather(row_pairs, "y"))
    row_pairs, col_pairs = lax.optimization_barrier((row_pairs, col_pairs))
    row_pairs = jnp.broadcast_to(row_pairs[None], (NX * NC, 16, 128))
    row_pairs = lax.all_to_all(row_pairs, ("x", "core"), 0, 0, tiled=True)

    block = (lax.axis_index("x") * NC + lax.axis_index("core")) * NY + lax.axis_index("y")
    ids = (block * SUB + jnp.arange(SUB, dtype=jnp.int32)).astype(f32)[None]
    dlogits, terms = call(
        passage_kernel,
        [shape(bf16, TALL, 384), shape(bf16, NZ, 112, 128)],
        placed,
        passage_part,
        targets,
        ids,
        row_pairs,
        col_pairs,
        far_outs=(1,),
        scratch=[
            pltpu.VMEM((4 * NY * SLICE, 128), f32),
            pltpu.VMEM((NZ, 112, 128), bf16),
            pltpu.SemaphoreType.DMA((NZ // 4,)),
        ],
        flops=2 * TALL * SUB * NC * THIRD,
    )
    terms = lax.all_to_all(terms, "z", 0, 0, tiled=True)
    dlogits, other_half = lax.optimization_barrier((dlogits, other_half))
    other_half = around(other_half, "core", NC, 1)

    own, *others = call(
        query_kernel,
        [shape(f32, 3 * ROWS, 128)] + [shape(bf16, 3 * ROWS, 128)] * (NX - 1),
        where,
        dlogits,
        around(dlogits, "core", NC, 1),
        own_half,
        other_half,
        scratch=[pltpu.VMEM((TALL, HALF), f32)],
        flops=4 * TALL * SUB * HALF,
    )
    came = [around(other, "x", NX, step) for step, other in enumerate(others, 1)]

    (message,) = call(
        fold_kernel,
        [shape(f32, NY, ROWS, 128)],
        terms,
        own,
        *came,
        scratch=[pltpu.VMEM((112, 128), f32), pltpu.VMEM((ROWS, 128), f32)],
    )
    message = lax.all_to_all(message, "y", 0, 0, tiled=True)
    query_grad, passage_grad = call(
        final_kernel,
        [shape(f32, ROWS, WIDTH), shape(f32, SLICE, COLS)],
        message,
        scratch=[pltpu.VMEM((3 * QUARTER, 128), f32)],
    )
    return (query_grad, passage_grad.T)


def solution(mesh):
    chips = Mesh(mesh.devices.reshape(NY, NZ, NX, NC), ("y", "z", "x", "core"))
    yz, xc = ("y", "z"), ("x", "core")
    return jax.shard_map(
        body,
        mesh=chips,
        in_specs=(P(yz, xc), P(xc, yz), P(yz)),
        out_specs=(P(yz, xc), P(xc, yz)),
        check_vma=False,
    )
```

```python
import jax
import jax.numpy as jnp
import numpy as np
from jax import lax
from jax.experimental import pallas as pl
from jax.experimental.pallas import tpu as pltpu
from jax.sharding import Mesh, PartitionSpec as P

logit_scale = 20.0
f32 = jnp.float32
bf16 = jnp.bfloat16
NY, NZ, NX, NC = 4, 16, 4, 2
ROWS, WIDTH = 144, 96
COLS, SLICE = 1152, 12
TALL, SUB = NY * ROWS, COLS // NY
HALF = NX * 128
THIRD = NZ * NY * SLICE // NC
BLOCKS = [(0, 128), (128, 128), (256, 128), (384, 128), (512, 64)]
MSG = ROWS + 48
QUARTER = ROWS // 4
STEPS = (2, 1, 3)
GROUP = 384
NT = (((1,), (1,)), ((), ()))
TN = (((0,), (0,)), ((), ()))


def call(kernel, outs, *args, far=(), far_outs=(), scratch=(), flops=0):
    bytes_accessed = sum(int(np.prod(a.shape)) * a.dtype.itemsize for a in (*args, *outs))
    vmem, smem, hbm = (pl.BlockSpec(memory_space=m) for m in (pltpu.VMEM, pltpu.SMEM, pltpu.HBM))
    return pl.pallas_call(
        kernel,
        out_shape=[pltpu.HBM(o.shape, o.dtype) if i in far_outs else o for i, o in enumerate(outs)],
        in_specs=[hbm if i in far else smem if a.ndim == 1 else vmem for i, a in enumerate(args)],
        out_specs=[hbm if i in far_outs else vmem for i in range(len(outs))],
        scratch_shapes=list(scratch),
        compiler_params=pltpu.CompilerParams(vmem_limit_bytes=32 << 20),
        cost_estimate=pl.CostEstimate(flops=flops, bytes_accessed=bytes_accessed, transcendentals=0),
    )(*(pltpu.with_memory_space_constraint(a, pltpu.HBM) if i in far else a for i, a in enumerate(args)))


def shape(dtype, *dims):
    return jax.ShapeDtypeStruct(dims, dtype)


def placement():
    table = np.zeros((NX, 128, NZ // NC, NY, SLICE), np.float32)
    for x in range(NX):
        for lane in range(WIDTH):
            table[x, lane, lane // SLICE, x, lane % SLICE] = 1.0
    return table.reshape(HALF, THIRD)


def columns(wide, width):
    lane = lax.broadcasted_iota(jnp.int32, (128, 128), 1)
    packed = jnp.ones((128, 128), f32)
    for j, group in enumerate(wide):
        for g, column in enumerate(group):
            if column.shape[0] < 128:
                column = jnp.concatenate([column, jnp.ones((128 - column.shape[0], 1), f32)], axis=0)
            packed = jnp.where(lane == 8 * g + j, column, packed)
    return packed.T[:width]


def upright(lines):
    return jnp.concatenate([lines, jnp.zeros((120, 128), f32)], axis=0).T


def prep_kernel(queries_in, positive_in, passages_in, message, queries, positive, passages, wide, tall, sems):
    pairs = ((queries_in, queries), (positive_in, positive), (passages_in, passages))
    copies = [pltpu.make_async_copy(a, b, sems.at[i]) for i, (a, b) in enumerate(pairs)]
    for copy in copies:
        copy.start()
    for copy in copies:
        copy.wait()
    index = positive[...].astype(f32)
    index = jnp.concatenate(
        [index[:, :128], jnp.concatenate([index[:, 128:], jnp.zeros((1, 256 - ROWS), f32)], axis=1)], axis=0
    )
    index = upright(jnp.concatenate([index, jnp.zeros((6, 128), f32)], axis=0))
    index = jnp.concatenate([index[:, 0:1], index[: ROWS - 128, 1:2]], axis=0)
    high = jnp.floor(index * (1.0 / 128.0))
    low = index - 128.0 * high
    wide[...] = jnp.zeros((ROWS, 128), f32)
    wide[:, :WIDTH] = queries[...].astype(f32)
    lane = lax.broadcasted_iota(jnp.int32, (ROWS, 128), 1)
    own = jnp.where(lane == WIDTH, high, jnp.where(lane == WIDTH + 1, low, wide[...])).astype(bf16)
    tall[...] = jnp.zeros((16, COLS), f32)
    tall[:SLICE] = passages[...].astype(f32)
    for y in range(NY):
        message[y, :ROWS] = own
        piece = pltpu.roll(tall[...], (COLS - y * SUB) % COLS, 1)
        for b in range(3):
            message[y, ROWS + 16 * b : ROWS + 16 * b + 16] = piece[:, b * 128 : (b + 1) * 128].astype(bf16)


def split_kernel(came, queries, part, staged, total, sems):
    for y in range(NY):
        staged[y * ROWS : (y + 1) * ROWS] = came[y, :ROWS]
    copies = [pltpu.make_async_copy(staged, queries.at[i], sems.at[i]) for i in range(NX * NC)]
    for copy in copies:
        copy.start()
    for y in range(NY):
        for b in range(3):
            piece = came[y, ROWS + 16 * b : ROWS + 16 * b + 16].astype(f32)
            total[y * SLICE : (y + 1) * SLICE, b * 128 : (b + 1) * 128] = piece[:SLICE]
    high = NY * SLICE
    for b in range(2):
        part[b * high : (b + 1) * high] = total[:, b * 128 : (b + 1) * 128].astype(bf16)
    lane = lax.broadcasted_iota(jnp.int32, (SLICE, 128), 1)
    tail = jnp.zeros((SLICE, 128), f32)
    for y in range(NY):
        piece = jnp.where(lane < SUB - 256, total[y * SLICE : (y + 1) * SLICE, 256:], 0.0)
        tail += piece if y == 0 else pltpu.roll(piece, 32 * y, 1)
    tail = jnp.concatenate([tail, jnp.zeros((16 - SLICE, 128), f32)], axis=0)
    part[2 * high :] = tail.astype(bf16)
    for copy in copies:
        copy.wait()


def unpack(came, passages, tails):
    high = NY * SLICE
    for z in range(NZ):
        for b in range(2):
            passages[z * high : (z + 1) * high, b * 128 : (b + 1) * 128] = came[z, b * high : (b + 1) * high]
    packed = came[:, 2 * high :].astype(f32).reshape(NZ * 16, 128)
    for y in range(NY):
        moved = packed if y == 0 else pltpu.roll(packed, 128 - 32 * y, 1)
        for z in range(NZ):
            tails[z * high + y * SLICE : z * high + (y + 1) * SLICE] = moved[z * 16 : z * 16 + SLICE]
    passages[:, 256:] = tails[:, : SUB - 256].astype(bf16)


def tile_kernel(
    parts, came, place, passages, row_pairs, col_pairs, placed, targets, query_half, logits, tails, rows, cols, sems
):
    unpack(came, passages, tails)
    for c in range(NC):
        for x in range(NX):
            query_half[:, x * 128 : (x + 1) * 128] = parts[c * NX + x]
        placed[:, c * THIRD : (c + 1) * THIRD] = jnp.dot(
            query_half[...], place[...], preferred_element_type=f32
        ).astype(bf16)
    pairs, col_top = [], None
    for start, size in BLOCKS:
        scores = logit_scale * jnp.dot(
            placed[start : start + size], passages[...], preferred_element_type=f32
        )
        logits[start : start + size] = scores
        top = jnp.max(scores, axis=1, keepdims=True)
        pairs.append((top, jnp.sum(jnp.exp(scores - top), axis=1, keepdims=True)))
        peak = jnp.max(scores, axis=0, keepdims=True)
        col_top = peak if col_top is None else jnp.maximum(col_top, peak)
    rows[...] = columns(pairs, 16)
    copies = [pltpu.make_async_copy(rows, row_pairs.at[i], sems.at[i]) for i in range(NX * NC)]
    for copy in copies:
        copy.start()
    col_sum = jnp.zeros((1, SUB), f32)
    for start, size in BLOCKS:
        col_sum += jnp.sum(jnp.exp(logits[start : start + size] - col_top), axis=0, keepdims=True)
    fill = jnp.ones((1, 384 - SUB), f32)
    both = [jnp.concatenate([v, fill], axis=1) for v in (col_top, col_sum)]
    lines = [v[:, b * 128 : (b + 1) * 128] for v in both for b in range(3)]
    cols[...] = jnp.concatenate(lines + [jnp.ones((2, 128), f32)], axis=0)
    for i in range(NZ):
        copies.append(pltpu.make_async_copy(cols, col_pairs.at[i], sems.at[NX * NC + i]))
        copies[-1].start()
    spare = parts[0].astype(f32)
    target = spare[:, WIDTH : WIDTH + 1] * 128.0 + spare[:, WIDTH + 1 : WIDTH + 2]
    targets[...] = columns([(target[start : start + size],) for start, size in BLOCKS], 8)
    for copy in copies:
        copy.wait()


def spread_kernel(where, passages, place, own_half, other_half):
    for c, half in ((where[0], own_half), (1 - where[0], other_half)):
        rows = pl.ds(pl.multiple_of(c * THIRD, THIRD), THIRD)
        half[...] = jnp.dot(place[...], passages[rows], preferred_element_type=f32).astype(bf16)


def passage_kernel(placed, passages, targets, ids, row_pairs, col_pairs, dlogits, out, tails, terms, sems):
    top, total = row_pairs[:, :8], row_pairs[:, 8:]
    peak = jnp.max(top, axis=0)
    row_lse = upright(peak + jnp.log(jnp.sum(total * jnp.exp(top - peak[None]), axis=0)))
    target = upright(targets[...])
    pairs = col_pairs[...]
    top, total = pairs[:, 0:3], pairs[:, 3:6]
    peak = jnp.max(top, axis=0)
    col_lse = peak + jnp.log(jnp.sum(total * jnp.exp(top - peak[None]), axis=0))
    col_lse = jnp.concatenate([col_lse[b : b + 1] for b in range(3)], axis=1)[:, :SUB]
    dlogits[:, 256:] = jnp.zeros((TALL, 128), bf16)
    for j, (start, size) in enumerate(BLOCKS):
        scores = logit_scale * jnp.dot(placed[start : start + size], passages[...], preferred_element_type=f32)
        slope = jnp.exp(scores - row_lse[:size, j : j + 1]) + jnp.exp(scores - col_lse)
        hit = jnp.where(target[:size, j : j + 1] == ids[...], 2.0, 0.0)
        dlogits[start : start + size, :SUB] = (slope - hit).astype(bf16)
    high = NY * SLICE
    copies = []
    for first in range(0, NZ, 4):
        if first * high % GROUP == 0:
            whole = logit_scale * lax.dot_general(
                placed[:, first * high : first * high + GROUP], dlogits[...], TN, preferred_element_type=f32
            )
        offset = first * high % GROUP
        part = whole[offset : offset + 4 * high]
        tails[...] = part[:, 256:]
        for i in range(4):
            for b in range(2):
                piece = part[i * high : (i + 1) * high, b * 128 : (b + 1) * 128]
                terms[first + i, b * high : (b + 1) * high] = piece.astype(bf16)
            tail = jnp.zeros((16, 128), f32)
            for a in range(NY):
                first_row = i * high + a * SLICE
                piece = jnp.concatenate([tails[first_row : first_row + SLICE], jnp.zeros((16 - SLICE, 128), f32)], axis=0)
                tail += piece if a == 0 else pltpu.roll(piece, 32 * a, 1)
            terms[first + i, 2 * high : 2 * high + 16] = tail.astype(bf16)
        group = pl.ds(first, 4)
        copies.append(pltpu.make_async_copy(terms.at[group], out.at[group], sems.at[first // 4]))
        copies[-1].start()
    for copy in copies:
        copy.wait()


def squeeze(block):
    lane = lax.broadcasted_iota(jnp.int32, (ROWS, 128), 1)
    tail = block[3 * ROWS :]
    parts = []
    for j in range(3):
        moved = pltpu.roll(tail, WIDTH - 32 * j, 1)
        parts.append(jnp.where(lane < WIDTH, block[j * ROWS : (j + 1) * ROWS], moved))
    return jnp.concatenate(parts, axis=0)


def query_kernel(where, dlogits, other_dlogits, own_half, other_half, own, *rest):
    outs, total = rest[:-1], rest[-1]
    total[...] = logit_scale * (
        lax.dot_general(dlogits[:, :SUB], own_half[...], NT, preferred_element_type=f32)
        + lax.dot_general(other_dlogits[:, :SUB], other_half[...], NT, preferred_element_type=f32)
    )
    own[...] = squeeze(total[:, pl.ds(pl.multiple_of(where[1] * 128, 128), 128)])
    for step, out in zip(STEPS, outs):
        lanes = pl.ds(pl.multiple_of(lax.rem(where[1] + step, NX) * 128, 128), 128)
        out[...] = squeeze(total[:, lanes]).astype(bf16)


def fold_kernel(terms, own, *rest):
    came, message, total, block = rest[:-3], rest[-3], rest[-2], rest[-1]
    high = NY * SLICE
    total[...] = jnp.sum(terms[...].astype(f32), axis=0)
    lane = lax.broadcasted_iota(jnp.int32, (ROWS, 128), 1)
    short = lax.broadcasted_iota(jnp.int32, (QUARTER, 128), 1)
    last = jnp.zeros((ROWS, 128), f32)
    for y in range(NY):
        if y < 3:
            rows = slice(y * ROWS, (y + 1) * ROWS)
            value = own[rows] + sum(c[rows].astype(f32) for c in came)
            moved = pltpu.roll(value, (128 + 32 * y - WIDTH) % 128, 1)
            last = jnp.where((lane >= 32 * y) & (lane < 32 * y + 32), moved, last)
        else:
            value = last
        block[...] = value
        extra = block[3 * QUARTER :]
        for j in range(3):
            moved = pltpu.roll(extra, WIDTH - 32 * j, 1)
            piece = block[j * QUARTER : (j + 1) * QUARTER]
            message[y, j * QUARTER : (j + 1) * QUARTER] = jnp.where(short < WIDTH, piece, moved)
        tail = total[2 * high :]
        tail = tail if y == 0 else pltpu.roll(tail, 128 - 32 * y, 1)
        for b in range(3):
            piece = tail[:SLICE] if b == 2 else total[b * high + y * SLICE : b * high + (y + 1) * SLICE]
            message[y, 3 * QUARTER + b * SLICE : 3 * QUARTER + (b + 1) * SLICE] = piece


def final_kernel(came, query_grad, passage_grad, total):
    total[...] = jnp.sum(came[:, : 3 * QUARTER], axis=0)
    short = lax.broadcasted_iota(jnp.int32, (QUARTER, 128), 1)
    last = jnp.zeros((QUARTER, 128), f32)
    for j in range(3):
        rows = slice(j * QUARTER, (j + 1) * QUARTER)
        query_grad[rows] = total[rows, :WIDTH]
        moved = pltpu.roll(total[rows], (128 + 32 * j - WIDTH) % 128, 1)
        last = jnp.where((short >= 32 * j) & (short < 32 * j + 32), moved, last)
    query_grad[3 * QUARTER :] = last[:, :WIDTH]
    lane = lax.broadcasted_iota(jnp.int32, (SLICE, 128), 1)
    wide = None
    for y in range(NY):
        first = 3 * QUARTER
        blocks = [came[y, first + b * SLICE : first + (b + 1) * SLICE] for b in range(3)]
        blocks[2] = jnp.where(lane < SUB - 256, blocks[2], 0.0)
        row = jnp.concatenate(blocks + [jnp.zeros((SLICE, COLS - 384), f32)], axis=1)
        row = jnp.concatenate([row, jnp.zeros((16 - SLICE, COLS), f32)], axis=0)
        row = row if y == 0 else pltpu.roll(row, y * SUB, 1)
        wide = row if wide is None else wide + row
    passage_grad[...] = wide[:SLICE]


def merge(pairs):
    top, total = pairs[:, :8], pairs[:, 8:]
    peak = jnp.max(top, axis=0)
    return jnp.concatenate([peak, jnp.sum(total * jnp.exp(top - peak[None]), axis=0)])


def around(x, axis, n, step):
    return lax.ppermute(x, axis, [(i, (i + step) % n) for i in range(n)])


def body(queries, passages, positive):
    place = jnp.asarray(placement(), bf16)
    where = jnp.stack([lax.axis_index("core"), lax.axis_index("x")]).astype(jnp.int32)

    (message,) = call(
        prep_kernel,
        [shape(bf16, NY, MSG, 128)],
        queries,
        positive[None],
        passages.T,
        far=(0, 1, 2),
        scratch=[
            pltpu.VMEM((ROWS, WIDTH), bf16),
            pltpu.VMEM((1, ROWS), jnp.int32),
            pltpu.VMEM((SLICE, COLS), bf16),
            pltpu.VMEM((ROWS, 128), f32),
            pltpu.VMEM((16, COLS), f32),
            pltpu.SemaphoreType.DMA((3,)),
        ],
    )
    message = lax.all_to_all(message, "y", 0, 0, tiled=True)
    parts, passage_part = call(
        split_kernel,
        [shape(bf16, NX * NC, TALL, 128), shape(bf16, 112, 128)],
        message,
        far_outs=(0,),
        scratch=[
            pltpu.VMEM((TALL, 128), bf16),
            pltpu.VMEM((NY * SLICE, 384), f32),
            pltpu.SemaphoreType.DMA((NX * NC,)),
        ],
    )
    parts = lax.all_to_all(parts, ("core", "x"), 0, 0, tiled=True)
    passage_part = lax.all_gather(passage_part, "z")

    passage_part, row_pairs, col_pairs, placed, targets = call(
        tile_kernel,
        [
            shape(bf16, NC * THIRD, SUB),
            shape(f32, NX * NC, 16, 128),
            shape(f32, NZ, 8, 128),
            shape(bf16, TALL, NC * THIRD),
            shape(f32, 8, 128),
        ],
        parts,
        passage_part,
        place,
        scratch=[
            pltpu.VMEM((TALL, HALF), bf16),
            pltpu.VMEM((TALL, SUB), f32),
            pltpu.VMEM((NC * THIRD, 128), f32),
            pltpu.VMEM((16, 128), f32),
            pltpu.VMEM((8, 128), f32),
            pltpu.SemaphoreType.DMA((NX * NC + NZ,)),
        ],
        far_outs=(1, 2),
        flops=2 * TALL * SUB * NC * HALF,
    )
    own_half, other_half = call(
        spread_kernel,
        [shape(bf16, HALF, SUB)] * 2,
        where,
        passage_part,
        place,
        flops=2 * NC * HALF * THIRD * SUB,
    )
    other_half = around(other_half, "core", NC, 1)
    col_pairs, own_half = lax.optimization_barrier((col_pairs, own_half))
    targets, other_half = lax.optimization_barrier((targets, other_half))
    row_pairs = lax.all_to_all(row_pairs, ("x", "core"), 0, 0, tiled=True)
    col_pairs = lax.all_to_all(col_pairs, "z", 0, 0, tiled=True)
    row_pairs = lax.all_gather(merge(row_pairs), "y")

    block = (lax.axis_index("x") * NC + lax.axis_index("core")) * NY + lax.axis_index("y")
    ids = (block * SUB + jnp.arange(SUB, dtype=jnp.int32)).astype(f32)[None]
    dlogits, terms = call(
        passage_kernel,
        [shape(bf16, TALL, 384), shape(bf16, NZ, 112, 128)],
        placed,
        passage_part,
        targets,
        ids,
        row_pairs,
        col_pairs,
        far_outs=(1,),
        scratch=[
            pltpu.VMEM((4 * NY * SLICE, 128), f32),
            pltpu.VMEM((NZ, 112, 128), bf16),
            pltpu.SemaphoreType.DMA((NZ // 4,)),
        ],
        flops=2 * TALL * SUB * NC * THIRD,
    )
    terms = lax.all_to_all(terms, "z", 0, 0, tiled=True)

    own, *others = call(
        query_kernel,
        [shape(f32, 3 * ROWS, 128)] + [shape(bf16, 3 * ROWS, 128)] * (NX - 1),
        where,
        dlogits,
        around(dlogits, "core", NC, 1),
        own_half,
        other_half,
        scratch=[pltpu.VMEM((TALL, HALF), f32)],
        flops=4 * TALL * SUB * HALF,
    )
    came = [around(other, "x", NX, step) for step, other in zip(STEPS, others)]

    (message,) = call(
        fold_kernel,
        [shape(f32, NY, ROWS, 128)],
        terms,
        own,
        *came,
        scratch=[pltpu.VMEM((112, 128), f32), pltpu.VMEM((ROWS, 128), f32)],
    )
    message = lax.all_to_all(message, "y", 0, 0, tiled=True)
    query_grad, passage_grad = call(
        final_kernel,
        [shape(f32, ROWS, WIDTH), shape(f32, SLICE, COLS)],
        message,
        scratch=[pltpu.VMEM((3 * QUARTER, 128), f32)],
    )
    return (query_grad, passage_grad.T)


def solution(mesh):
    chips = Mesh(mesh.devices.reshape(NY, NZ, NX, NC), ("y", "z", "x", "core"))
    yz, xc = ("y", "z"), ("x", "core")
    return jax.shard_map(
        body,
        mesh=chips,
        in_specs=(P(yz, xc), P(xc, yz), P(yz)),
        out_specs=(P(yz, xc), P(xc, yz)),
        check_vma=False,
    )
```
